512 devices in a mesh: dp: 16 (over z_lo, x), panel: 32 (over y, z_hi, core).
Axes of the slice: x: 4, y: 4, z: 16 (z_hi: 4, z_lo: 4; z = z_hi * 4 + z_lo), core: 2. Of those that a mesh axis runs over, the one named last changes fastest.
Arguments:
- features: bfloat16 [12288, 4096], P('dp', 'panel'), may hold values from -48 to 48
- sketch: float32 [32, 128, 256], P('panel', 'dp'), may hold values from -6 to 6
- counts: int32 [16], replicated, may hold values from 384 to 768, as said below
Outputs:
- covariance: float32 [4096, 16, 256], P('panel', 'dp')
- basis: float32 [32, 128, 256], P('panel', 'dp')
The draws below stay inside these ranges and needn't reach their ends.
Inputs may be any that keep to these rules, and one draw needn't show every extreme that they name: `counts`: some dp index has all 768 rows live.
All inputs are finite; a program needn't handle non-finite values.
Results may differ from the reference program's by a relative error of at most 0.0003.
Values may be sent and summed in bfloat16 or wider, within the bound.
No kernel may reach another device: no remote copies, remote signals or barrier semaphores. Data moves between devices by JAX's collectives and lax.ppermute only.
A program may use at most 64 MiB of HBM per device.

```python
import math
import jax
import jax.numpy as jnp
from jax import lax

D = 4096
RANK = 256
TOK_DEV = 768
ITERS = 2
TOKENS = 12288
PANEL_ROWS = 128
SUB = 8
N_DP = 16
N_PANEL = 32


def shard_counts(key):
    sub_key = jax.random.fold_in(key, 11)
    drawn = jax.random.randint(sub_key, (N_DP,), TOK_DEV // 2, TOK_DEV + 1)
    full_shard = jax.random.randint(jax.random.fold_in(sub_key, 1), (), 0, N_DP)
    return jnp.where(jnp.arange(N_DP) == full_shard, TOK_DEV, drawn).astype(jnp.int32)


def draw_counts(key, part):
    return shard_counts(key)


def draw_features(key, part):
    counts = shard_counts(key)
    key = jax.random.fold_in(key, 3)
    key_main, key_scale = jax.random.split(key, 2)
    column = jnp.arange(D, dtype=jnp.float32) / D
    feature_ramp = 0.7 + 0.7 * column
    spread = jnp.exp(jax.random.uniform(key_scale, (D,), jnp.float32, math.log(0.7), math.log(1.4)))
    base_draw = jnp.clip(jax.random.normal(key_main, (TOKENS, D), jnp.float32), -6.0, 6.0)
    values = base_draw * (feature_ramp * spread)[None, :]
    position = jnp.arange(TOKENS)
    live_rows = position % TOK_DEV < counts[position // TOK_DEV]
    values = jnp.where(live_rows[:, None], values, 4.0 * values)
    return values.astype(jnp.bfloat16)


def block_scale(key, shape, cuts, smallest, high):
    gain, own = 1.0, jax.random.fold_in(key, 6)
    for dim, parts in cuts:
        heights = jnp.exp(jax.random.uniform(jax.random.fold_in(own, dim), (parts,), jnp.float32, smallest / len(cuts), high / len(cuts)))
        gain = gain * jnp.repeat(heights, shape[dim] // parts).reshape([-1 if axis == dim else 1 for axis in range(len(shape))])
    return gain


def bell_draw(key, extent, scale, most, pieces=(), held_as=jnp.bfloat16):
    values = jax.random.normal(key, extent, jnp.float32) * scale
    if len(pieces) > 0:
        values = block_scale(key, extent, pieces, -0.22, 0.18) * values
    return jnp.clip(values, min=-most, max=most).astype(held_as)


def setup_inputs(seed: int = 0) -> dict:
    key_of = jax.random.split(jax.random.key(seed), 4)
    return {
        "features": draw_features(jax.random.fold_in(key_of[3], 71), 0),
        "sketch": bell_draw(key_of[1], (N_PANEL, PANEL_ROWS, RANK), 1.0, 6.0, ((0, 32), (1, 16)), jnp.float32),
        "counts": draw_counts(jax.random.fold_in(key_of[3], 71), 0),
    }


def reference(features, sketch, counts):
    position = jnp.arange(TOKENS, dtype=jnp.int32)
    live_rows = position % TOK_DEV < counts[position // TOK_DEV]
    wide_rows = features.astype(jnp.float32)
    masked = jnp.where(live_rows[:, None], wide_rows, jnp.zeros_like(wide_rows))
    token_total = jnp.sum(counts).astype(jnp.float32)
    gram_full = jnp.dot(masked.T.astype(jnp.float32), wide_rows.astype(jnp.float32), precision=lax.Precision.HIGHEST, preferred_element_type=jnp.float32)
    covariance = gram_full / token_total
    basis_now = sketch.reshape(D, RANK)
    for sweep in range(ITERS):
        product = jnp.dot(covariance.astype(jnp.float32), basis_now.astype(jnp.float32), precision=lax.Precision.HIGHEST, preferred_element_type=jnp.float32)
        inner_gram = jnp.dot(product.T.astype(jnp.float32), product.astype(jnp.float32), precision=lax.Precision.HIGHEST, preferred_element_type=jnp.float32)
        factor_low = jnp.linalg.cholesky(inner_gram)
        basis_now = jax.scipy.linalg.solve_triangular(factor_low, product.T, lower=True).T
    scaled = (math.sqrt(D) * basis_now).reshape(N_PANEL, D // N_PANEL, RANK)
    stored = covariance.reshape(D, N_PANEL, N_DP, SUB).transpose(0, 2, 1, 3).reshape(D, N_DP, N_PANEL * SUB)
    return (stored, scaled)
```

```python
import math

import jax
import jax.numpy as jnp
from jax import lax
from jax.experimental import pallas as pl
from jax.experimental.pallas import tpu as pltpu
from jax.sharding import Mesh, PartitionSpec as P

F32 = jnp.float32
BF16 = jnp.bfloat16
HIGH = lax.Precision.HIGHEST
DP = ("zl", "x")
PANEL = ("y", "zh", "c")
YC = ("y", "c")
STEP = 32


def exchange(blocks, axes):
    return lax.all_to_all(blocks, axes, 0, 0, tiled=True)


def gather(block, axes):
    size = lax.axis_size(axes)
    return exchange(jnp.broadcast_to(block[None], (size,) + block.shape), axes)


def solve_kernel(gram_ref, rows_ref, out_ref, held_ref):
    rank = gram_ref.shape[0]
    width = held_ref.shape[1]
    held_ref[:, 0:rank] = gram_ref[...]
    held_ref[:, rank:width] = rows_ref[...]
    index = lax.broadcasted_iota(jnp.int32, (STEP, 1), 0)
    for first in range(0, rank, STEP):
        left = first // 128 * 128
        panel = held_ref[first : first + STEP, left:width]
        if first > 0:
            panel = panel - lax.dot_general(
                held_ref[0:first, first : first + STEP],
                held_ref[0:first, left:width],
                (((0,), (0,)), ((), ())),
                precision=HIGH,
                preferred_element_type=F32,
            )
        pivots = jnp.ones((STEP, 1), F32)
        for step in range(STEP):
            at = first + step - left
            column = panel[:, at : at + 1]
            pivot = column[step : step + 1, :]
            factor = jnp.where(index > step, column / pivot, 0.0)
            pivots = jnp.where(index == step, pivot, pivots)
            panel = panel - factor * panel[step : step + 1, :]
        held_ref[first : first + STEP, left:width] = panel * (1.0 / jnp.sqrt(pivots))
    out_ref[...] = held_ref[:, rank:width]


def solve(gram, rows):
    count, rank = rows.shape
    padded = jnp.pad(rows.T, ((0, 0), (0, 128 - count)))
    solved = pl.pallas_call(
        solve_kernel,
        out_shape=jax.ShapeDtypeStruct((rank, 128), F32),
        scratch_shapes=[pltpu.VMEM((rank, rank + 128), F32)],
        name="solve",
    )(gram, padded)
    return solved[:, 0:count].T


def local(features, sketch, counts):
    tok_rows, width = features.shape
    sub_rows, rank = sketch.shape[1:]
    n_dp, n_panel = lax.axis_size(DP), lax.axis_size(PANEL)
    n_y, n_zh, n_c = lax.axis_size("y"), lax.axis_size("zh"), lax.axis_size("c")
    limit = counts[lax.axis_index(DP)]
    masked = jnp.where(lax.iota(jnp.int32, tok_rows)[:, None] < limit, features, 0)
    token_total = jnp.sum(counts).astype(F32)

    high = lax.reduce_precision(sketch[0], 8, 7)
    rest = sketch[0] - high
    middle = lax.reduce_precision(rest, 8, 7)
    extra = jnp.stack([high, middle, rest - middle]).astype(BF16).reshape(-1, width)
    extra_rows = extra.shape[0]

    along_z = gather(jnp.concatenate([masked, extra]), ("zh",))
    along_y = gather(
        jnp.concatenate([masked, along_z[:, tok_rows:].reshape(-1, width)]), ("y",)
    )
    along_c = gather(along_y, ("c",))

    thirds = along_c[:, :, tok_rows:].astype(F32)
    thirds = thirds.reshape(n_c, n_y, n_zh, 3, sub_rows, rank)
    start = (thirds[:, :, :, 0] + thirds[:, :, :, 1]) + thirds[:, :, :, 2]
    start = start.transpose(1, 2, 0, 3, 4).reshape(n_panel * sub_rows, rank)

    partial_sums = jnp.einsum(
        "ztf,cyta->zfcya",
        along_z[:, :tok_rows],
        along_c[:, :, :tok_rows],
        preferred_element_type=F32,
    )
    partial_sums = partial_sums.reshape(n_zh, n_dp, sub_rows, n_c, n_y, width)
    partial_sums = partial_sums.transpose(1, 4, 3, 0, 2, 5)
    partial_sums = partial_sums.reshape(n_dp * n_y * n_c, n_zh, sub_rows, width)
    received = exchange(partial_sums, DP + YC)
    received = received.reshape(n_dp, n_y, n_c, n_zh, sub_rows, width)
    columns = jnp.sum(received, axis=0).transpose(0, 2, 1, 3, 4)
    columns = columns.reshape(n_panel * sub_rows, width) / token_total
    covariance = columns.T.reshape(width, 1, n_panel * sub_rows)

    product = lax.dot_general(
        columns, start, (((0,), (0,)), ((), ())), precision=HIGH, preferred_element_type=F32
    )
    product = jnp.sum(exchange(product.reshape(n_dp, sub_rows, rank), DP), axis=0)
    product = gather(product, DP).reshape(width, rank)
    product = jnp.dot(columns, product, precision=HIGH, preferred_element_type=F32)
    rows = jnp.sum(exchange(product.reshape(n_panel, sub_rows, rank), PANEL), axis=0)

    group = gather(rows, PANEL).reshape(n_panel * sub_rows, rank)
    gram = lax.dot_general(
        group, group, (((0,), (0,)), ((), ())), precision=HIGH, preferred_element_type=F32
    )
    gram = jnp.sum(exchange(gram.reshape(n_dp, -1, rank), DP), axis=0)
    gram = gather(gram, DP).reshape(rank, rank)
    basis = math.sqrt(width * n_panel) * solve(gram, rows)
    return covariance, basis[None]


def solution(mesh):
    inner = Mesh(mesh.devices.reshape(4, 4, 4, 4, 2), DP + PANEL)
    return jax.shard_map(
        local,
        mesh=inner,
        in_specs=(P(DP, PANEL), P(PANEL, DP, None), P()),
        out_specs=(P(PANEL, DP, None), P(PANEL, DP, None)),
        check_vma=False,
    )
```

```python
import math

import jax
import jax.numpy as jnp
from jax import lax
from jax.experimental import pallas as pl
from jax.experimental.pallas import tpu as pltpu
from jax.sharding import Mesh, PartitionSpec as P

F32 = jnp.float32
HIGH = lax.Precision.HIGHEST
DP = ("zl", "x")
PANEL = ("y", "zh", "c")
YC = ("y", "c")
XYC = ("x", "y", "c")
STEP = 32
PAD_ROWS = 24


def exchange(blocks, axes):
    return lax.all_to_all(blocks, axes, 0, 0, tiled=True)


def gather(block, axes):
    size = lax.axis_size(axes)
    return exchange(jnp.broadcast_to(block[None], (size,) + block.shape), axes)


def solve_kernel(gram_ref, rows_ref, out_ref, held_ref):
    rank = gram_ref.shape[0]
    width = held_ref.shape[1]
    held_ref[:, 0:rank] = gram_ref[...]
    held_ref[:, rank:width] = rows_ref[...]
    index = lax.broadcasted_iota(jnp.int32, (STEP, 1), 0)
    for first in range(0, rank, STEP):
        left = first // 128 * 128
        panel = held_ref[first : first + STEP, left:width]
        if first > 0:
            panel = panel - lax.dot_general(
                held_ref[0:first, first : first + STEP],
                held_ref[0:first, left:width],
                (((0,), (0,)), ((), ())),
                precision=HIGH,
                preferred_element_type=F32,
            )
        pivots = jnp.ones((STEP, 1), F32)
        for step in range(STEP):
            at = first + step - left
            column = panel[:, at : at + 1]
            pivot = column[step : step + 1, :]
            factor = jnp.where(index > step, column / pivot, 0.0)
            pivots = jnp.where(index == step, pivot, pivots)
            panel = panel - factor * panel[step : step + 1, :]
        held_ref[first : first + STEP, left:width] = panel * (1.0 / jnp.sqrt(pivots))
    out_ref[...] = held_ref[:, rank:width]


def solve(gram, rows):
    count, rank = rows.shape
    padded = jnp.pad(rows.T, ((0, 0), (0, 128 - count)))
    solved = pl.pallas_call(
        solve_kernel,
        out_shape=jax.ShapeDtypeStruct((rank, 128), F32),
        scratch_shapes=[pltpu.VMEM((rank, rank + 128), F32)],
        name="solve",
    )(gram, padded)
    return solved[:, 0:count].T


def local(features, sketch, counts):
    tok_rows, width = features.shape
    sub_rows, rank = sketch.shape[1:]
    n_dp, n_panel = lax.axis_size(DP), lax.axis_size(PANEL)
    n_zl, n_x, n_y, n_zh, n_c = (lax.axis_size(name) for name in DP + PANEL)
    limit = counts[lax.axis_index(DP)]
    masked = jnp.where(lax.iota(jnp.int32, tok_rows)[:, None] < limit, features, 0)
    token_total = jnp.sum(counts).astype(F32)

    along_z = gather(features, ("zh",))
    across = lax.all_gather(masked, YC)
    wide = jnp.pad(sketch[0], ((0, PAD_ROWS), (0, 0)))
    start = lax.all_gather(wide, PANEL)[:, 0:sub_rows].reshape(n_panel * sub_rows, rank)

    sums = jnp.einsum("ztf,pta->zfpa", along_z, across, preferred_element_type=F32)
    sums = sums.reshape(n_zh, n_zl, n_x, sub_rows, n_y * n_c, width)
    sums = sums.transpose(2, 4, 1, 0, 3, 5)
    sums = sums.reshape(n_x * n_y * n_c, n_zl, n_zh, sub_rows, width)
    sums = exchange(sums, XYC).reshape(n_x, n_y * n_c, n_zl, n_zh, sub_rows, width)
    sums = jnp.sum(sums, axis=0).transpose(1, 0, 2, 3, 4)
    sums = jnp.sum(exchange(sums, ("zl",)), axis=0)
    columns = sums.reshape(n_y, n_c, n_zh, sub_rows, width).transpose(0, 2, 1, 3, 4)
    columns = columns.reshape(n_panel * sub_rows, width) / token_total
    covariance = columns.T.reshape(width, 1, n_panel * sub_rows)

    product = lax.dot_general(
        columns, start, (((0,), (0,)), ((), ())), precision=HIGH, preferred_element_type=F32
    )
    product = jnp.sum(exchange(product.reshape(n_dp, sub_rows, rank), DP), axis=0)
    product = gather(product, DP).reshape(width, rank)
    product = jnp.dot(columns, product, precision=HIGH, preferred_element_type=F32)
    rows = jnp.sum(exchange(product.reshape(n_panel, sub_rows, rank), PANEL), axis=0)

    group = gather(rows, PANEL).reshape(n_panel * sub_rows, rank)
    gram = lax.dot_general(
        group, group, (((0,), (0,)), ((), ())), precision=HIGH, preferred_element_type=F32
    )
    gram = jnp.sum(exchange(gram.reshape(n_dp, -1, rank), DP), axis=0)
    gram = gather(gram, DP).reshape(rank, rank)
    basis = math.sqrt(width * n_panel) * solve(gram, rows)
    return covariance, basis[None]


def solution(mesh):
    inner = Mesh(mesh.devices.reshape(4, 4, 4, 4, 2), DP + PANEL)
    return jax.shard_map(
        local,
        mesh=inner,
        in_specs=(P(DP, PANEL), P(PANEL, DP, None), P()),
        out_specs=(P(PANEL, DP, None), P(PANEL, DP, None)),
        check_vma=False,
    )
```

```python
import math

import jax
import jax.numpy as jnp
from jax import lax
from jax.experimental import pallas as pl
from jax.experimental.pallas import tpu as pltpu
from jax.sharding import Mesh, PartitionSpec as P

F32 = jnp.float32
BF16 = jnp.bfloat16
HIGH = lax.Precision.HIGHEST
DP = ("zl", "x")
PANEL = ("y", "zh", "c")
YC = ("y", "c")
XYC = ("x", "y", "c")
PANEL_STEP = 64
BLOCK = 8
PAD_ROWS = 512


def exchange(blocks, axes):
    return lax.all_to_all(blocks, axes, 0, 0, tiled=True)


def gather(block, axes):
    size = lax.axis_size(axes)
    return exchange(jnp.broadcast_to(block[None], (size,) + block.shape), axes)


def solve_kernel(gram_ref, rows_ref, out_ref, held_ref):
    rank, lanes = rows_ref.shape
    width = held_ref.shape[1]
    held_ref[:, 0:rank] = gram_ref[...]
    held_ref[:, rank:width] = rows_ref[...]
    for first in range(0, rank, PANEL_STEP):
        last = first + PANEL_STEP
        parts = {}
        for at in range(first // lanes * lanes, width, lanes):
            parts[at] = held_ref[first:last, at : at + lanes]
            if first > 0:
                parts[at] = parts[at] - lax.dot_general(
                    held_ref[0:first, first:last],
                    held_ref[0:first, at : at + lanes],
                    (((0,), (0,)), ((), ())),
                    precision=HIGH,
                    preferred_element_type=F32,
                )
        for pivot in range(first, last, BLOCK):
            base = pivot // lanes * lanes
            parts = {at: part for at, part in parts.items() if at >= base}
            source, lane = parts[base], pivot - base
            columns = [
                jnp.broadcast_to(source[:, lane + j : lane + j + 1], source.shape)
                for j in range(BLOCK)
            ]
            square = [[columns[j][i : i + 1] for j in range(i + 1)] for i in range(BLOCK)]
            rows = [{at: part[j : j + 1] for at, part in parts.items()} for j in range(BLOCK)]
            inverse = []
            for j in range(BLOCK):
                inverse.append(1.0 / square[j][j])
                for i in range(j + 1, BLOCK):
                    factor = square[i][j] * inverse[j]
                    for m in range(j + 1, i + 1):
                        square[i][m] = square[i][m] - factor * square[m][j]
                    for at in parts:
                        rows[i][at] = rows[i][at] - factor * rows[j][at]
                    if pivot + BLOCK < last:
                        columns[i] = columns[i] - columns[j] * factor
            for j in range(BLOCK):
                scale = 1.0 / jnp.sqrt(square[j][j])
                for at in parts:
                    held_ref[pivot + j : pivot + j + 1, at : at + lanes] = rows[j][at] * scale
            if pivot + BLOCK < last:
                for at in parts:
                    rest = parts[at][BLOCK:]
                    for j in range(BLOCK):
                        rest = rest - columns[j][BLOCK:] * (rows[j][at] * inverse[j])
                    parts[at] = rest
    out_ref[...] = held_ref[:, rank:width]


def solve(gram, rows):
    count, rank = rows.shape
    padded = jnp.pad(rows.T, ((0, 0), (0, 128 - count)))
    solved = pl.pallas_call(
        solve_kernel,
        out_shape=jax.ShapeDtypeStruct((rank, 128), F32),
        scratch_shapes=[pltpu.VMEM((rank, rank + 128), F32)],
        name="solve",
    )(gram, padded)
    return solved[:, 0:count].T


def local(features, sketch, counts):
    tok_rows, width = features.shape
    sub_rows, rank = sketch.shape[1:]
    n_dp, n_panel = lax.axis_size(DP), lax.axis_size(PANEL)
    n_zl, n_x, n_y, n_zh, n_c = (lax.axis_size(name) for name in DP + PANEL)
    limit = counts[lax.axis_index(DP)]
    live = lax.iota(jnp.int32, tok_rows)[:, None] < limit
    token_total = jnp.sum(counts).astype(F32)

    high = lax.reduce_precision(sketch[0], 8, 7)
    rest = sketch[0] - high
    middle = lax.reduce_precision(rest, 8, 7)
    extra = jnp.stack([high, middle, rest - middle]).astype(BF16).reshape(-1, width)

    across = lax.all_gather(features, YC)
    along_z = lax.all_gather(jnp.concatenate([features, extra]), "zh")
    thirds = along_z[:, tok_rows:].reshape(-1, width)
    thirds = lax.all_gather(jnp.pad(thirds, ((0, PAD_ROWS - thirds.shape[0]), (0, 0))), YC)
    thirds = thirds[:, 0 : n_zh * extra.shape[0]].astype(F32)
    thirds = thirds.reshape(n_y * n_c, n_zh, 3, sub_rows, rank)
    start = (thirds[:, :, 0] + thirds[:, :, 1]) + thirds[:, :, 2]
    start = start.reshape(n_panel * sub_rows, rank)

    near = jnp.where(live, along_z[:, :tok_rows], 0)
    sums = jnp.einsum("ztf,pta->zfpa", near, across, preferred_element_type=F32)
    sums = sums.reshape(n_zh, n_zl, n_x, sub_rows, n_y * n_c, width)
    sums = sums.transpose(2, 4, 1, 0, 3, 5)
    sums = sums.reshape(n_x * n_y * n_c, n_zl, n_zh, sub_rows, width)
    sums = exchange(sums, XYC).reshape(n_x, n_y * n_c, n_zl, n_zh, sub_rows, width)
    sums = jnp.sum(sums, axis=0).transpose(1, 0, 2, 3, 4)
    sums = jnp.sum(exchange(sums, ("zl",)), axis=0) / token_total

    columns = sums.reshape(n_panel * sub_rows, width)
    covariance = sums.reshape(n_y, n_c, n_zh, sub_rows, width)
    covariance = covariance.transpose(4, 0, 2, 1, 3).reshape(width, 1, n_panel * sub_rows)

    product = lax.dot_general(
        columns, start, (((0,), (0,)), ((), ())), precision=HIGH, preferred_element_type=F32
    )
    product = jnp.sum(exchange(product.reshape(n_dp, sub_rows, rank), DP), axis=0)
    product = gather(product, DP).reshape(width, rank)
    product = jnp.dot(columns, product, precision=HIGH, preferred_element_type=F32)
    rows = jnp.sum(exchange(product.reshape(n_y * n_c, n_zh * sub_rows, rank), YC), axis=0)
    rows = jnp.sum(gather(rows, ("zh",)), axis=0)

    gram = lax.dot_general(
        rows, rows, (((0,), (0,)), ((), ())), precision=HIGH, preferred_element_type=F32
    )
    gram = jnp.sum(exchange(gram.reshape(n_x * n_y * n_c, -1, rank), XYC), axis=0)
    gram = jnp.sum(gather(gram, ("zl",)), axis=0)
    gram = gather(gram, XYC).reshape(rank, rank)
    own = lax.dynamic_slice_in_dim(rows, lax.axis_index("zh") * sub_rows, sub_rows)
    basis = math.sqrt(width * n_panel) * solve(gram, own)
    return covariance, basis[None]


def solution(mesh):
    inner = Mesh(mesh.devices.reshape(4, 4, 4, 4, 2), DP + PANEL)
    return jax.shard_map(
        local,
        mesh=inner,
        in_specs=(P(DP, PANEL), P(PANEL, DP, None), P()),
        out_specs=(P(PANEL, DP, None), P(PANEL, DP, None)),
        check_vma=False,
    )
```

```python
import math

import jax
import jax.numpy as jnp
from jax import lax
from jax.experimental import pallas as pl
from jax.experimental.pallas import tpu as pltpu
from jax.sharding import Mesh, PartitionSpec as P

F32 = jnp.float32
BF16 = jnp.bfloat16
HIGH = lax.Precision.HIGHEST
DP = ("zl", "x")
PANEL = ("y", "zh", "c")
YC = ("y", "c")
XYC = ("x", "y", "c")
ZYC = ("zl", "y", "c")
PANEL_STEP = 64
BLOCK = 8


def exchange(blocks, axes):
    return lax.all_to_all(blocks, axes, 0, 0, tiled=True)


def gather(block, axes):
    size = lax.axis_size(axes)
    return exchange(jnp.broadcast_to(block[None], (size,) + block.shape), axes)


def solve_kernel(gram_ref, rows_ref, out_ref, held_ref):
    rank, lanes = rows_ref.shape
    width = held_ref.shape[1]
    held_ref[:, 0:rank] = gram_ref[...]
    held_ref[:, rank:width] = rows_ref[...]
    for first in range(0, rank, PANEL_STEP):
        last = first + PANEL_STEP
        parts = {}
        for at in range(first // lanes * lanes, width, lanes):
            parts[at] = held_ref[first:last, at : at + lanes]
            if first > 0:
                parts[at] = parts[at] - lax.dot_general(
                    held_ref[0:first, first:last],
                    held_ref[0:first, at : at + lanes],
                    (((0,), (0,)), ((), ())),
                    precision=HIGH,
                    preferred_element_type=F32,
                )
        for pivot in range(first, last, BLOCK):
            base = pivot // lanes * lanes
            parts = {at: part for at, part in parts.items() if at >= base}
            source, lane = parts[base], pivot - base
            columns = [
                jnp.broadcast_to(source[:, lane + j : lane + j + 1], source.shape)
                for j in range(BLOCK)
            ]
            square = [[columns[j][i : i + 1] for j in range(i + 1)] for i in range(BLOCK)]
            rows = [{at: part[j : j + 1] for at, part in parts.items()} for j in range(BLOCK)]
            inverse = []
            for j in range(BLOCK):
                inverse.append(1.0 / square[j][j])
                for i in range(j + 1, BLOCK):
                    factor = square[i][j] * inverse[j]
                    for m in range(j + 1, i + 1):
                        square[i][m] = square[i][m] - factor * square[m][j]
                    for at in parts:
                        rows[i][at] = rows[i][at] - factor * rows[j][at]
                    if pivot + BLOCK < last:
                        columns[i] = columns[i] - columns[j] * factor
            for j in range(BLOCK):
                scale = 1.0 / jnp.sqrt(square[j][j])
                for at in parts:
                    held_ref[pivot + j : pivot + j + 1, at : at + lanes] = rows[j][at] * scale
            if pivot + BLOCK < last:
                for at in parts:
                    rest = parts[at][BLOCK:]
                    for j in range(BLOCK):
                        rest = rest - columns[j][BLOCK:] * (rows[j][at] * inverse[j])
                    parts[at] = rest
    out_ref[...] = held_ref[:, rank:width]


def solve(gram, rows):
    count, rank = rows.shape
    padded = jnp.pad(rows.T, ((0, 0), (0, 128 - count)))
    solved = pl.pallas_call(
        solve_kernel,
        out_shape=jax.ShapeDtypeStruct((rank, 128), F32),
        scratch_shapes=[pltpu.VMEM((rank, rank + 128), F32)],
        name="solve",
    )(gram, padded)
    return solved[:, 0:count].T


def local(features, sketch, counts):
    tok_rows, width = features.shape
    sub_rows, rank = sketch.shape[1:]
    n_dp, n_panel = lax.axis_size(DP), lax.axis_size(PANEL)
    n_zl, n_x, n_y, n_zh, n_c = (lax.axis_size(name) for name in DP + PANEL)
    limit = counts[lax.axis_index(DP)]
    live = lax.iota(jnp.int32, tok_rows)[:, None] < limit
    token_total = jnp.sum(counts).astype(F32)

    high = lax.reduce_precision(sketch[0], 8, 7)
    rest = sketch[0] - high
    middle = lax.reduce_precision(rest, 8, 7)
    extra = jnp.stack([high, middle, rest - middle]).astype(BF16).reshape(-1, width)

    across = lax.all_gather(features, YC)
    along_z = lax.all_gather(jnp.concatenate([features, extra]), "zh")
    thirds = along_z[:, tok_rows:].reshape(-1, width)
    thirds = lax.all_gather(thirds, ZYC).astype(F32)
    thirds = thirds.reshape(n_zl * n_y * n_c, n_zh, 3, sub_rows, rank)
    start = (thirds[:, :, 0] + thirds[:, :, 1]) + thirds[:, :, 2]
    start = start.reshape(n_zl * n_panel * sub_rows, rank)

    near = jnp.where(live, along_z[:, :tok_rows], 0)
    sums = jnp.einsum("ztf,pta->zfpa", near, across, preferred_element_type=F32)
    sums = sums.reshape(n_zh, n_zl, n_x, sub_rows, n_y * n_c, width)
    sums = sums.transpose(2, 4, 1, 0, 3, 5)
    sums = sums.reshape(n_x * n_y * n_c, n_zl, n_zh, sub_rows, width)
    sums = exchange(sums, XYC).reshape(n_x, n_y * n_c, n_zl, n_zh, sub_rows, width)
    sums = jnp.sum(sums, axis=0).transpose(1, 0, 2, 3, 4)

    product = lax.dot_general(
        sums.reshape(-1, width), start, (((0,), (0,)), ((), ())), precision=HIGH, preferred_element_type=F32
    )
    product = product.reshape(n_zl, width // n_zl, rank // width, width).transpose(0, 2, 1, 3)
    group_rows = n_panel * sub_rows
    both = [sums.reshape(n_zl, group_rows, width), product.reshape(n_zl, -1, width)]
    both = jnp.sum(exchange(jnp.concatenate(both, axis=1), ("zl",)), axis=0) / token_total
    product = jnp.sum(gather(both[group_rows:], ("x",)), axis=0)
    product = gather(product, ("zl",)).reshape(n_zl, rank // width, width // n_zl, width)
    product = product.transpose(0, 2, 1, 3).reshape(width, rank)

    columns = both[:group_rows]
    covariance = columns.reshape(n_y, n_c, n_zh, sub_rows, width)
    covariance = covariance.transpose(4, 0, 2, 1, 3).reshape(width, 1, group_rows)

    product = jnp.dot(columns, product, precision=HIGH, preferred_element_type=F32)
    rows = jnp.sum(exchange(product.reshape(n_y * n_c, n_zh * sub_rows, rank), YC), axis=0)
    rows = jnp.sum(gather(rows, ("zh",)), axis=0)

    gram = lax.dot_general(
        rows, rows, (((0,), (0,)), ((), ())), precision=HIGH, preferred_element_type=F32
    )
    gram = jnp.sum(exchange(gram.reshape(n_x * n_y * n_c, -1, rank), XYC), axis=0)
    gram = jnp.sum(gather(gram, ("zl",)), axis=0)
    gram = gather(gram, XYC).reshape(rank, rank)
    own = lax.dynamic_slice_in_dim(rows, lax.axis_index("zh") * sub_rows, sub_rows)
    basis = math.sqrt(width * n_panel) * solve(gram, own)
    return covariance, basis[None]


def solution(mesh):
    inner = Mesh(mesh.devices.reshape(4, 4, 4, 4, 2), DP + PANEL)
    return jax.shard_map(
        local,
        mesh=inner,
        in_specs=(P(DP, PANEL), P(PANEL, DP, None), P()),
        out_specs=(P(PANEL, DP, None), P(PANEL, DP, None)),
        check_vma=False,
    )
```

```python
import functools
import math

import jax
import jax.numpy as jnp
from jax import lax
from jax.experimental import pallas as pl
from jax.experimental.pallas import tpu as pltpu
from jax.sharding import Mesh, PartitionSpec as P

F32 = jnp.float32
BF16 = jnp.bfloat16
HIGH = lax.Precision.HIGHEST
DP = ("zl", "x")
PANEL = ("y", "zh", "c")
YC = ("y", "c")
XYC = ("x", "y", "c")
PANEL_STEP = 64
BLOCK = 8
PAD_ROWS = 512


def exchange(blocks, axes):
    return lax.all_to_all(blocks, axes, 0, 0, tiled=True)


def gather(block, axes):
    size = lax.axis_size(axes)
    return exchange(jnp.broadcast_to(block[None], (size,) + block.shape), axes)


def solve_kernel(place_ref, gram_ref, rows_ref, out_ref, held_ref, *, scale_by):
    count, rank = out_ref.shape
    width = held_ref.shape[1]
    lanes = width - rank
    own = rows_ref[pl.ds(pl.multiple_of(place_ref[0] * count, count), count), :]
    padded = jnp.concatenate([own, jnp.zeros((lanes - count, rank), F32)], axis=0)
    held_ref[:, 0:rank] = gram_ref[...]
    held_ref[:, rank:width] = padded.T
    for first in range(0, rank, PANEL_STEP):
        last = first + PANEL_STEP
        parts = {}
        for at in range(first // lanes * lanes, width, lanes):
            parts[at] = held_ref[first:last, at : at + lanes]
            if first > 0:
                parts[at] = parts[at] - lax.dot_general(
                    held_ref[0:first, first:last],
                    held_ref[0:first, at : at + lanes],
                    (((0,), (0,)), ((), ())),
                    precision=HIGH,
                    preferred_element_type=F32,
                )
        for pivot in range(first, last, BLOCK):
            base = pivot // lanes * lanes
            parts = {at: part for at, part in parts.items() if at >= base}
            source, lane = parts[base], pivot - base
            columns = [
                jnp.broadcast_to(source[:, lane + j : lane + j + 1], source.shape)
                for j in range(BLOCK)
            ]
            square = [[columns[j][i : i + 1] for j in range(i + 1)] for i in range(BLOCK)]
            rows = [{at: part[j : j + 1] for at, part in parts.items()} for j in range(BLOCK)]
            inverse = []
            for j in range(BLOCK):
                inverse.append(1.0 / square[j][j])
                for i in range(j + 1, BLOCK):
                    factor = square[i][j] * inverse[j]
                    for m in range(j + 1, i + 1):
                        square[i][m] = square[i][m] - factor * square[m][j]
                    for at in parts:
                        rows[i][at] = rows[i][at] - factor * rows[j][at]
                    if pivot + BLOCK < last:
                        columns[i] = columns[i] - columns[j] * factor
            for j in range(BLOCK):
                scale = 1.0 / jnp.sqrt(square[j][j])
                for at in parts:
                    held_ref[pivot + j : pivot + j + 1, at : at + lanes] = rows[j][at] * scale
            if pivot + BLOCK < last:
                for at in parts:
                    rest = parts[at][BLOCK:]
                    for j in range(BLOCK):
                        rest = rest - columns[j][BLOCK:] * (rows[j][at] * inverse[j])
                    parts[at] = rest
    out_ref[...] = held_ref[:, rank:width].T[0:count] * scale_by


def solve(gram, rows, place, count, scale_by):
    rank = rows.shape[1]
    vmem = pl.BlockSpec(memory_space=pltpu.VMEM)
    return pl.pallas_call(
        functools.partial(solve_kernel, scale_by=scale_by),
        out_shape=jax.ShapeDtypeStruct((count, rank), F32),
        in_specs=[pl.BlockSpec(memory_space=pltpu.SMEM), vmem, vmem],
        out_specs=vmem,
        scratch_shapes=[pltpu.VMEM((rank, rank + 128), F32)],
        name="solve",
    )(place, gram, rows)


def tile_kernel(limit_ref, near_ref, across_ref, out_ref, turned_ref):
    n_zh, width = near_ref.shape[0], near_ref.shape[2]
    tok_rows = across_ref.shape[1]
    n_x, pair, n_zl, _, sub_rows, _ = out_ref.shape

    @pl.when(pl.program_id(0) == 0)
    def turn():
        token = lax.broadcasted_iota(jnp.int32, (tok_rows, width), 0)
        live = jnp.where(token < limit_ref[0], 1.0, 0.0)
        for z in range(n_zh):
            kept = near_ref[z, 0:tok_rows, :].astype(F32) * live
            turned_ref[z * width : (z + 1) * width, :] = kept.astype(BF16).T

    both = jnp.concatenate([across_ref[p] for p in range(pair)], axis=1)
    for z in range(n_zh):
        product = jnp.dot(
            turned_ref[z * width : (z + 1) * width, :], both, preferred_element_type=F32
        )
        for low in range(n_zl):
            for x in range(n_x):
                row = (low * n_x + x) * sub_rows
                for p in range(pair):
                    out_ref[x, p, low, z] = product[row : row + sub_rows, p * width : (p + 1) * width]


def tile(limit, near, across, n_zl, n_x, sub_rows):
    n_zh, near_rows, width = near.shape
    panels, tok_rows = across.shape[:2]
    return pl.pallas_call(
        tile_kernel,
        grid=(panels // 2,),
        out_shape=jax.ShapeDtypeStruct((n_x, panels, n_zl, n_zh, sub_rows, width), F32),
        in_specs=[
            pl.BlockSpec(memory_space=pltpu.SMEM),
            pl.BlockSpec((n_zh, near_rows, width), lambda q: (0, 0, 0)),
            pl.BlockSpec((2, tok_rows, width), lambda q: (q, 0, 0)),
        ],
        out_specs=pl.BlockSpec((n_x, 2, n_zl, n_zh, sub_rows, width), lambda q: (0, q, 0, 0, 0, 0)),
        scratch_shapes=[pltpu.VMEM((n_zh * width, tok_rows), BF16)],
        name="tile",
    )(limit, near, across)


def local(features, sketch, counts):
    tok_rows, width = features.shape
    sub_rows, rank = sketch.shape[1:]
    n_dp, n_panel = lax.axis_size(DP), lax.axis_size(PANEL)
    n_zl, n_x, n_y, n_zh, n_c = (lax.axis_size(name) for name in DP + PANEL)
    limit = lax.dynamic_slice_in_dim(counts, lax.axis_index(DP), 1)
    token_total = jnp.sum(counts).astype(F32)

    high = lax.reduce_precision(sketch[0], 8, 7)
    rest = sketch[0] - high
    middle = lax.reduce_precision(rest, 8, 7)
    extra = jnp.stack([high, middle, rest - middle]).astype(BF16).reshape(-1, width)

    across = lax.all_gather(features, YC)
    along_z = lax.all_gather(jnp.concatenate([features, extra]), "zh")
    thirds = along_z[:, tok_rows:].reshape(-1, width)
    thirds = lax.all_gather(jnp.pad(thirds, ((0, PAD_ROWS - thirds.shape[0]), (0, 0))), YC)
    thirds = thirds[:, 0 : n_zh * extra.shape[0]].astype(F32)
    thirds = thirds.reshape(n_y * n_c, n_zh, 3, sub_rows, rank)
    start = (thirds[:, :, 0] + thirds[:, :, 1]) + thirds[:, :, 2]
    start = start.reshape(n_panel * sub_rows, rank)

    sums = tile(limit, along_z, across, n_zl, n_x, sub_rows)
    sums = sums.reshape(n_x * n_y * n_c, n_zl, n_zh, sub_rows, width)
    sums = exchange(sums, XYC).reshape(n_x, n_y * n_c, n_zl, n_zh, sub_rows, width)
    sums = jnp.sum(sums, axis=0).transpose(1, 0, 2, 3, 4)
    sums = jnp.sum(exchange(sums, ("zl",)), axis=0) / token_total

    columns = sums.reshape(n_panel * sub_rows, width)
    covariance = sums.reshape(n_y, n_c, n_zh, sub_rows, width)
    covariance = covariance.transpose(4, 0, 2, 1, 3).reshape(width, 1, n_panel * sub_rows)

    product = lax.dot_general(
        columns, start, (((0,), (0,)), ((), ())), precision=HIGH, preferred_element_type=F32
    )
    product = jnp.sum(exchange(product.reshape(n_dp, sub_rows, rank), DP), axis=0)
    product = gather(product, DP).reshape(width, rank)
    product = jnp.dot(columns, product, precision=HIGH, preferred_element_type=F32)
    rows = jnp.sum(exchange(product.reshape(n_y * n_c, n_zh * sub_rows, rank), YC), axis=0)
    rows = jnp.sum(lax.all_gather(rows, "zh"), axis=0)

    gram = lax.dot_general(
        rows, rows, (((0,), (0,)), ((), ())), precision=HIGH, preferred_element_type=F32
    )
    gram = jnp.sum(exchange(gram.reshape(n_x * n_y * n_c, -1, rank), XYC), axis=0)
    gram = jnp.sum(gather(gram, ("zl",)), axis=0)
    gram = gather(gram, XYC).reshape(rank, rank)
    place = lax.axis_index("zh").reshape(1)
    basis = solve(gram, rows, place, sub_rows, math.sqrt(width * n_panel))
    return covariance, basis[None]


def solution(mesh):
    inner = Mesh(mesh.devices.reshape(4, 4, 4, 4, 2), DP + PANEL)
    return jax.shard_map(
        local,
        mesh=inner,
        in_specs=(P(DP, PANEL), P(PANEL, DP, None), P()),
        out_specs=(P(PANEL, DP, None), P(PANEL, DP, None)),
        check_vma=False,
    )
```

```python
import functools
import math

import jax
import jax.numpy as jnp
from jax import lax
from jax.experimental import pallas as pl
from jax.experimental.pallas import tpu as pltpu
from jax.sharding import Mesh, PartitionSpec as P

F32 = jnp.float32
BF16 = jnp.bfloat16
HIGH = lax.Precision.HIGHEST
DP = ("zl", "x")
PANEL = ("y", "zh", "c")
YC = ("y", "c")
XYC = ("x", "y", "c")
RAISE = 256.0
PANEL_STEP = 64
BLOCK = 8
PAD_ROWS = 512


def exchange(blocks, axes):
    return lax.all_to_all(blocks, axes, 0, 0, tiled=True)


def gather(block, axes):
    size = lax.axis_size(axes)
    return exchange(jnp.broadcast_to(block[None], (size,) + block.shape), axes)


def solve_kernel(place_ref, gram_ref, rows_ref, out_ref, held_ref, *, scale_by):
    count, rank = out_ref.shape
    width = held_ref.shape[1]
    lanes = width - rank
    own = rows_ref[pl.ds(pl.multiple_of(place_ref[0] * count, count), count), :]
    gram = gram_ref[...]
    diagonal = lax.broadcasted_iota(jnp.int32, gram.shape, 0) == lax.broadcasted_iota(
        jnp.int32, gram.shape, 1
    )
    kept = jnp.where(diagonal, gram, 0.0)
    down = 1.0 / jnp.sqrt(jnp.sum(kept, axis=1, keepdims=True))
    along = 1.0 / jnp.sqrt(jnp.sum(kept, axis=0, keepdims=True))
    own = jnp.concatenate([own * along, jnp.zeros((lanes - count, rank), F32)], axis=0)
    held_ref[:, 0:rank] = gram * down * along
    held_ref[:, rank:width] = own.T
    for first in range(0, rank, PANEL_STEP):
        last = first + PANEL_STEP
        parts = {}
        for at in range(first // lanes * lanes, width, lanes):
            parts[at] = held_ref[first:last, at : at + lanes]
            if first > 0:
                parts[at] = parts[at] - lax.dot_general(
                    held_ref[0:first, first:last],
                    held_ref[0:first, at : at + lanes],
                    (((0,), (0,)), ((), ())),
                    precision=HIGH,
                    preferred_element_type=F32,
                )
        for pivot in range(first, last, BLOCK):
            base = pivot // lanes * lanes
            parts = {at: part for at, part in parts.items() if at >= base}
            source, lane = parts[base], pivot - base
            columns = [
                jnp.broadcast_to(source[:, lane + j : lane + j + 1], source.shape)
                for j in range(BLOCK)
            ]
            square = [[columns[j][i : i + 1] for j in range(i + 1)] for i in range(BLOCK)]
            rows = [{at: part[j : j + 1] for at, part in parts.items()} for j in range(BLOCK)]
            inverse = []
            for j in range(BLOCK):
                if j % 2 == 0:
                    top, cross, corner = square[j][j], square[j + 1][j], square[j + 1][j + 1]
                    inverse.append(1.0 / top)
                    inverse.append(top * (1.0 / (top * corner - cross * cross)))
                for i in range(j + 1, BLOCK):
                    factor = square[i][j] * inverse[j]
                    for m in range(j + 1, i + 1):
                        square[i][m] = square[i][m] - factor * square[m][j]
                    for at in parts:
                        rows[i][at] = rows[i][at] - factor * rows[j][at]
                    if pivot + BLOCK < last:
                        columns[i] = columns[i] - columns[j] * factor
            for j in range(BLOCK):
                scale = 1.0 / jnp.sqrt(square[j][j])
                for at in parts:
                    held_ref[pivot + j : pivot + j + 1, at : at + lanes] = rows[j][at] * scale
            if pivot + BLOCK < last:
                for at in parts:
                    rest = parts[at][BLOCK:]
                    for j in range(BLOCK):
                        rest = rest - columns[j][BLOCK:] * (rows[j][at] * inverse[j])
                    parts[at] = rest
    out_ref[...] = held_ref[:, rank:width].T[0:count] * scale_by


def solve(gram, rows, place, count, scale_by):
    rank = rows.shape[1]
    vmem = pl.BlockSpec(memory_space=pltpu.VMEM)
    return pl.pallas_call(
        functools.partial(solve_kernel, scale_by=scale_by),
        out_shape=jax.ShapeDtypeStruct((count, rank), F32),
        in_specs=[pl.BlockSpec(memory_space=pltpu.SMEM), vmem, vmem],
        out_specs=vmem,
        scratch_shapes=[pltpu.VMEM((rank, rank + 128), F32)],
        name="solve",
    )(place, gram, rows)


def tile_kernel(place_ref, counts_ref, near_ref, across_ref, out_ref, turned_ref):
    n_zh, width = near_ref.shape[0], near_ref.shape[2]
    tok_rows = across_ref.shape[1]
    n_x, pair, n_zl, _, sub_rows, _ = out_ref.shape

    @pl.when(pl.program_id(0) == 0)
    def turn():
        token = lax.broadcasted_iota(jnp.int32, (width, tok_rows), 1)
        live = jnp.where(token < counts_ref[place_ref[0]], 1.0, 0.0).astype(BF16)
        for z in range(n_zh):
            turned_ref[z * width : (z + 1) * width, :] = near_ref[z, 0:tok_rows, :].T * live

    both = jnp.concatenate([across_ref[p] for p in range(pair)], axis=1)
    product = jnp.dot(turned_ref[...], both, preferred_element_type=F32)
    for z in range(n_zh):
        for low in range(n_zl):
            for x in range(n_x):
                row = ((z * n_zl + low) * n_x + x) * sub_rows
                for p in range(pair):
                    out_ref[x, p, low, z] = product[row : row + sub_rows, p * width : (p + 1) * width]


def tile(place, counts, near, across, n_zl, n_x, sub_rows):
    n_zh, near_rows, width = near.shape
    panels, tok_rows = across.shape[:2]
    return pl.pallas_call(
        tile_kernel,
        grid=(panels // 2,),
        out_shape=jax.ShapeDtypeStruct((n_x, panels, n_zl, n_zh, sub_rows, width), F32),
        in_specs=[
            pl.BlockSpec(memory_space=pltpu.SMEM),
            pl.BlockSpec(memory_space=pltpu.SMEM),
            pl.BlockSpec((n_zh, near_rows, width), lambda q: (0, 0, 0)),
            pl.BlockSpec((2, tok_rows, width), lambda q: (q, 0, 0)),
        ],
        out_specs=pl.BlockSpec((n_x, 2, n_zl, n_zh, sub_rows, width), lambda q: (0, q, 0, 0, 0, 0)),
        scratch_shapes=[pltpu.VMEM((n_zh * width, tok_rows), BF16)],
        name="tile",
    )(place, counts, near, across)


def local(features, sketch, counts):
    tok_rows, width = features.shape
    sub_rows, rank = sketch.shape[1:]
    n_dp, n_panel = lax.axis_size(DP), lax.axis_size(PANEL)
    n_zl, n_x, n_y, n_zh, n_c = (lax.axis_size(name) for name in DP + PANEL)
    token_total = jnp.sum(counts).astype(F32)

    high = lax.reduce_precision(sketch[0], 8, 7)
    rest = sketch[0] - high
    middle = lax.reduce_precision(rest, 8, 7)
    extra = jnp.stack([high, middle, rest - middle]).astype(BF16).reshape(-1, width)

    across = lax.all_gather(features, YC)
    along_z = lax.all_gather(jnp.concatenate([features, extra]), "zh")
    thirds = along_z[:, tok_rows:].reshape(-1, width)
    thirds = lax.all_gather(jnp.pad(thirds, ((0, PAD_ROWS - thirds.shape[0]), (0, 0))), YC)
    thirds = thirds[:, 0 : n_zh * extra.shape[0]].astype(F32)
    thirds = thirds.reshape(n_y * n_c, n_zh, 3, sub_rows, rank)
    start = (thirds[:, :, 0] + thirds[:, :, 1]) + thirds[:, :, 2]
    start = start.reshape(n_panel * sub_rows, rank)

    sums = tile(lax.axis_index(DP).reshape(1), counts, along_z, across, n_zl, n_x, sub_rows)
    sums = sums.reshape(n_x * n_y * n_c, n_zl, n_zh, sub_rows, width)
    sums = exchange(sums, XYC).reshape(n_x, n_y * n_c, n_zl, n_zh, sub_rows, width)
    sums = jnp.sum(sums, axis=0).transpose(1, 0, 2, 3, 4)
    sums = jnp.sum(exchange(sums, ("zl",)), axis=0) / token_total

    columns = sums.reshape(n_panel * sub_rows, width)
    covariance = sums.reshape(n_y, n_c, n_zh, sub_rows, width)
    covariance = covariance.transpose(4, 0, 2, 1, 3).reshape(width, 1, n_panel * sub_rows)

    product = lax.dot_general(
        columns, start, (((0,), (0,)), ((), ())), precision=HIGH, preferred_element_type=F32
    )
    product = jnp.sum(exchange(product.reshape(n_dp, sub_rows, rank), DP), axis=0)
    product = gather(product, DP).reshape(width, rank)
    product = jnp.dot(columns, product, precision=HIGH, preferred_element_type=F32)
    rows = jnp.sum(exchange(product.reshape(n_y * n_c, n_zh * sub_rows, rank), YC), axis=0)
    rows = RAISE * jnp.sum(lax.all_gather(rows, "zh"), axis=0)

    gram = lax.dot_general(
        rows, rows, (((0,), (0,)), ((), ())), precision=HIGH, preferred_element_type=F32
    )
    gram = jnp.sum(exchange(gram.reshape(n_x * n_y * n_c, -1, rank), XYC), axis=0)
    gram = jnp.sum(gather(gram, ("zl",)), axis=0)
    gram = gather(gram, XYC).reshape(rank, rank)
    place = lax.axis_index("zh").reshape(1)
    basis = solve(gram, rows, place, sub_rows, math.sqrt(width * n_panel))
    return covariance, basis[None]


def solution(mesh):
    inner = Mesh(mesh.devices.reshape(4, 4, 4, 4, 2), DP + PANEL)
    return jax.shard_map(
        local,
        mesh=inner,
        in_specs=(P(DP, PANEL), P(PANEL, DP, None), P()),
        out_specs=(P(PANEL, DP, None), P(PANEL, DP, None)),
        check_vma=False,
    )
```

```python
import functools
import math

import jax
import jax.numpy as jnp
from jax import lax
from jax.experimental import pallas as pl
from jax.experimental.pallas import tpu as pltpu
from jax.sharding import Mesh, PartitionSpec as P

F32 = jnp.float32
BF16 = jnp.bfloat16
HIGH = lax.Precision.HIGHEST
DP = ("zl", "x")
PANEL = ("y", "zh", "c")
YC = ("y", "c")
XYC = ("x", "y", "c")
RAISE = 256.0
KERNEL_VMEM = 16 * 2**20
PANEL_STEP = 64
BLOCK = 8
PAD_ROWS = 512


def exchange(blocks, axes):
    return lax.all_to_all(blocks, axes, 0, 0, tiled=True)


def gather(block, axes):
    size = lax.axis_size(axes)
    return exchange(jnp.broadcast_to(block[None], (size,) + block.shape), axes)


def solve_kernel(place_ref, gram_ref, rows_ref, out_ref, held_ref, *, scale_by):
    count, rank = out_ref.shape
    width = held_ref.shape[1]
    lanes = width - rank
    own = rows_ref[pl.ds(pl.multiple_of(place_ref[0] * count, count), count), :]
    gram = gram_ref[...]
    diagonal = lax.broadcasted_iota(jnp.int32, gram.shape, 0) == lax.broadcasted_iota(
        jnp.int32, gram.shape, 1
    )
    kept = jnp.where(diagonal, gram, 0.0)
    down = 1.0 / jnp.sqrt(jnp.sum(kept, axis=1, keepdims=True))
    along = 1.0 / jnp.sqrt(jnp.sum(kept, axis=0, keepdims=True))
    own = jnp.concatenate([own * along, jnp.zeros((lanes - count, rank), F32)], axis=0)
    held_ref[:, 0:rank] = gram * down * along
    held_ref[:, rank:width] = own.T
    for first in range(0, rank, PANEL_STEP):
        last = first + PANEL_STEP
        parts = {}
        for at in range(first // lanes * lanes, width, lanes):
            parts[at] = held_ref[first:last, at : at + lanes]
            if first > 0:
                parts[at] = parts[at] - lax.dot_general(
                    held_ref[0:first, first:last],
                    held_ref[0:first, at : at + lanes],
                    (((0,), (0,)), ((), ())),
                    precision=HIGH,
                    preferred_element_type=F32,
                )
        for pivot in range(first, last, BLOCK):
            base = pivot // lanes * lanes
            parts = {at: part for at, part in parts.items() if at >= base}
            source, lane = parts[base], pivot - base
            columns = [
                jnp.broadcast_to(source[:, lane + j : lane + j + 1], source.shape)
                for j in range(BLOCK)
            ]
            square = [[columns[j][i : i + 1] for j in range(i + 1)] for i in range(BLOCK)]
            rows = [{at: part[j : j + 1] for at, part in parts.items()} for j in range(BLOCK)]
            inverse = []
            for j in range(BLOCK):
                if j % 2 == 0:
                    top, cross, corner = square[j][j], square[j + 1][j], square[j + 1][j + 1]
                    inverse.append(1.0 / top)
                    inverse.append(top * (1.0 / (top * corner - cross * cross)))
                for i in range(j + 1, BLOCK):
                    factor = square[i][j] * inverse[j]
                    for m in range(j + 1, i + 1):
                        square[i][m] = square[i][m] - factor * square[m][j]
                    for at in parts:
                        rows[i][at] = rows[i][at] - factor * rows[j][at]
                    if pivot + BLOCK < last:
                        columns[i] = columns[i] - columns[j] * factor
            for j in range(BLOCK):
                scale = 1.0 / jnp.sqrt(square[j][j])
                for at in parts:
                    held_ref[pivot + j : pivot + j + 1, at : at + lanes] = rows[j][at] * scale
            if pivot + BLOCK < last:
                for at in parts:
                    rest = parts[at][BLOCK:]
                    for j in range(BLOCK):
                        rest = rest - columns[j][BLOCK:] * (rows[j][at] * inverse[j])
                    parts[at] = rest
    out_ref[...] = held_ref[:, rank:width].T[0:count] * scale_by


def solve(gram, rows, place, count, scale_by):
    rank = rows.shape[1]
    vmem = pl.BlockSpec(memory_space=pltpu.VMEM)
    return pl.pallas_call(
        functools.partial(solve_kernel, scale_by=scale_by),
        out_shape=jax.ShapeDtypeStruct((count, rank), F32),
        in_specs=[pl.BlockSpec(memory_space=pltpu.SMEM), vmem, vmem],
        out_specs=vmem,
        scratch_shapes=[pltpu.VMEM((rank, rank + 128), F32)],
        compiler_params=pltpu.CompilerParams(vmem_limit_bytes=KERNEL_VMEM),
        name="solve",
    )(place, gram, rows)


def tile_kernel(place_ref, counts_ref, near_ref, across_ref, out_ref, turned_ref):
    n_zh, width = near_ref.shape[0], near_ref.shape[2]
    tok_rows = across_ref.shape[1]
    n_x, panels, n_zl, _, sub_rows, _ = out_ref.shape
    token = lax.broadcasted_iota(jnp.int32, (width, tok_rows), 1)
    live = jnp.where(token < counts_ref[place_ref[0]], 1.0, 0.0).astype(BF16)
    for z in range(n_zh):
        turned_ref[z * width : (z + 1) * width, :] = near_ref[z, 0:tok_rows, :].T * live
    beside = jnp.concatenate([across_ref[p] for p in range(panels)], axis=1)
    product = jnp.dot(turned_ref[...], beside, preferred_element_type=F32)
    for z in range(n_zh):
        for low in range(n_zl):
            for x in range(n_x):
                row = ((z * n_zl + low) * n_x + x) * sub_rows
                for p in range(panels):
                    out_ref[x, p, low, z] = product[row : row + sub_rows, p * width : (p + 1) * width]


def tile(place, counts, near, across, n_zl, n_x, sub_rows):
    n_zh, width = near.shape[0], near.shape[2]
    panels, tok_rows = across.shape[:2]
    smem = pl.BlockSpec(memory_space=pltpu.SMEM)
    vmem = pl.BlockSpec(memory_space=pltpu.VMEM)
    return pl.pallas_call(
        tile_kernel,
        out_shape=jax.ShapeDtypeStruct((n_x, panels, n_zl, n_zh, sub_rows, width), F32),
        in_specs=[smem, smem, vmem, vmem],
        out_specs=vmem,
        scratch_shapes=[pltpu.VMEM((n_zh * width, tok_rows), BF16)],
        compiler_params=pltpu.CompilerParams(vmem_limit_bytes=KERNEL_VMEM),
        name="tile",
    )(place, counts, near, across)


def local(features, sketch, counts):
    tok_rows, width = features.shape
    sub_rows, rank = sketch.shape[1:]
    n_dp, n_panel = lax.axis_size(DP), lax.axis_size(PANEL)
    n_zl, n_x, n_y, n_zh, n_c = (lax.axis_size(name) for name in DP + PANEL)
    token_total = jnp.sum(counts).astype(F32)

    high = lax.reduce_precision(sketch[0], 8, 7)
    rest = sketch[0] - high
    middle = lax.reduce_precision(rest, 8, 7)
    extra = jnp.stack([high, middle, rest - middle]).astype(BF16).reshape(-1, width)

    across = lax.all_gather(features, YC)
    along_z = lax.all_gather(jnp.concatenate([features, extra]), "zh")
    thirds = along_z[:, tok_rows:].reshape(-1, width)
    thirds = lax.all_gather(jnp.pad(thirds, ((0, PAD_ROWS - thirds.shape[0]), (0, 0))), YC)
    thirds = thirds[:, 0 : n_zh * extra.shape[0]].astype(F32)
    thirds = thirds.reshape(n_y * n_c, n_zh, 3, sub_rows, rank)
    start = (thirds[:, :, 0] + thirds[:, :, 1]) + thirds[:, :, 2]
    start = start.reshape(n_panel * sub_rows, rank)

    sums = tile(lax.axis_index(DP).reshape(1), counts, along_z, across, n_zl, n_x, sub_rows)
    sums = sums.reshape(n_x * n_y * n_c, n_zl, n_zh, sub_rows, width)
    sums = exchange(sums, XYC).reshape(n_x, n_y * n_c, n_zl, n_zh, sub_rows, width)
    sums = jnp.sum(sums, axis=0).transpose(1, 0, 2, 3, 4)
    sums = jnp.sum(exchange(sums, ("zl",)), axis=0) / token_total

    columns = sums.reshape(n_panel * sub_rows, width)
    covariance = sums.reshape(n_y, n_c, n_zh, sub_rows, width)
    covariance = covariance.transpose(4, 0, 2, 1, 3).reshape(width, 1, n_panel * sub_rows)

    product = lax.dot_general(
        columns, start, (((0,), (0,)), ((), ())), precision=HIGH, preferred_element_type=F32
    )
    product = jnp.sum(exchange(product.reshape(n_dp, sub_rows, rank), DP), axis=0)
    product = gather(product, DP).reshape(width, rank)
    product = jnp.dot(columns, product, precision=HIGH, preferred_element_type=F32)
    rows = jnp.sum(exchange(product.reshape(n_y * n_c, n_zh * sub_rows, rank), YC), axis=0)
    rows = RAISE * jnp.sum(lax.all_gather(rows, "zh"), axis=0)

    gram = lax.dot_general(
        rows, rows, (((0,), (0,)), ((), ())), precision=HIGH, preferred_element_type=F32
    )
    gram = jnp.sum(exchange(gram.reshape(n_x * n_y * n_c, -1, rank), XYC), axis=0)
    gram = jnp.sum(gather(gram, ("zl",)), axis=0)
    gram = gather(gram, XYC).reshape(rank, rank)
    place = lax.axis_index("zh").reshape(1)
    basis = solve(gram, rows, place, sub_rows, math.sqrt(width * n_panel))
    return covariance, basis[None]


def solution(mesh):
    inner = Mesh(mesh.devices.reshape(4, 4, 4, 4, 2), DP + PANEL)
    return jax.shard_map(
        local,
        mesh=inner,
        in_specs=(P(DP, PANEL), P(PANEL, DP, None), P()),
        out_specs=(P(PANEL, DP, None), P(PANEL, DP, None)),
        check_vma=False,
    )
```

```python
import functools
import math

import jax
import jax.numpy as jnp
from jax import lax
from jax.experimental import pallas as pl
from jax.experimental.pallas import tpu as pltpu
from jax.sharding import Mesh, PartitionSpec as P

F32 = jnp.float32
BF16 = jnp.bfloat16
HIGH = lax.Precision.HIGHEST
DP = ("zl", "x")
PANEL = ("y", "zh", "c")
YC = ("y", "c")
XYC = ("x", "y", "c")
RAISE = 256.0
KERNEL_VMEM = 16 * 2**20
PANEL_STEP = 64
BLOCK = 8
PAD_ROWS = 512


def exchange(blocks, axes):
    return lax.all_to_all(blocks, axes, 0, 0, tiled=True)


def gather(block, axes):
    size = lax.axis_size(axes)
    return exchange(jnp.broadcast_to(block[None], (size,) + block.shape), axes)


def solve_kernel(place_ref, gram_ref, rows_ref, out_ref, held_ref, *, scale_by):
    count, rank = out_ref.shape
    width = held_ref.shape[1]
    lanes = width - rank
    own = rows_ref[pl.ds(pl.multiple_of(place_ref[0] * count, count), count), :]
    gram = gram_ref[...]
    diagonal = lax.broadcasted_iota(jnp.int32, gram.shape, 0) == lax.broadcasted_iota(
        jnp.int32, gram.shape, 1
    )
    kept = jnp.where(diagonal, gram, 0.0)
    down = 1.0 / jnp.sqrt(jnp.sum(kept, axis=1, keepdims=True))
    along = 1.0 / jnp.sqrt(jnp.sum(kept, axis=0, keepdims=True))
    own = jnp.concatenate([own * along, jnp.zeros((lanes - count, rank), F32)], axis=0)
    held_ref[:, 0:rank] = gram * down * along
    held_ref[:, rank:width] = own.T
    for first in range(0, rank, PANEL_STEP):
        last = first + PANEL_STEP
        parts = {}
        for at in range(first // lanes * lanes, width, lanes):
            parts[at] = held_ref[first:last, at : at + lanes]
            if first > 0:
                parts[at] = parts[at] - lax.dot_general(
                    held_ref[0:first, first:last],
                    held_ref[0:first, at : at + lanes],
                    (((0,), (0,)), ((), ())),
                    precision=HIGH,
                    preferred_element_type=F32,
                )
        for pivot in range(first, last, BLOCK):
            base = pivot // lanes * lanes
            parts = {at: part for at, part in parts.items() if at >= base}
            source, lane = parts[base], pivot - base
            columns = [
                jnp.broadcast_to(source[:, lane + j : lane + j + 1], source.shape)
                for j in range(BLOCK)
            ]
            square = [[columns[j][i : i + 1] for j in range(i + 1)] for i in range(BLOCK)]
            rows = [{at: part[j : j + 1] for at, part in parts.items()} for j in range(BLOCK)]
            inverse = []
            for j in range(BLOCK):
                if j % 2 == 0:
                    top, cross, corner = square[j][j], square[j + 1][j], square[j + 1][j + 1]
                    inverse.append(1.0 / top)
                    inverse.append(top * (1.0 / (top * corner - cross * cross)))
                for i in range(j + 1, BLOCK):
                    factor = square[i][j] * inverse[j]
                    for m in range(j + 1, i + 1):
                        square[i][m] = square[i][m] - factor * square[m][j]
                    for at in parts:
                        rows[i][at] = rows[i][at] - factor * rows[j][at]
                    if pivot + BLOCK < last:
                        columns[i] = columns[i] - columns[j] * factor
            for j in range(BLOCK):
                scale = 1.0 / jnp.sqrt(square[j][j])
                for at in parts:
                    held_ref[pivot + j : pivot + j + 1, at : at + lanes] = rows[j][at] * scale
            if pivot + BLOCK < last:
                for at in parts:
                    rest = parts[at][BLOCK:]
                    for j in range(BLOCK):
                        rest = rest - columns[j][BLOCK:] * (rows[j][at] * inverse[j])
                    parts[at] = rest
    out_ref[...] = held_ref[:, rank:width].T[0:count] * scale_by


def solve(gram, rows, place, count, scale_by):
    rank = rows.shape[1]
    vmem = pl.BlockSpec(memory_space=pltpu.VMEM)
    return pl.pallas_call(
        functools.partial(solve_kernel, scale_by=scale_by),
        out_shape=jax.ShapeDtypeStruct((count, rank), F32),
        in_specs=[pl.BlockSpec(memory_space=pltpu.SMEM), vmem, vmem],
        out_specs=vmem,
        scratch_shapes=[pltpu.VMEM((rank, rank + 128), F32)],
        compiler_params=pltpu.CompilerParams(vmem_limit_bytes=KERNEL_VMEM),
        name="solve",
    )(place, gram, rows)


def tile_kernel(
    place_ref, counts_ref, near_any, across_any, out_any,
    near_ref, across_ref, out_ref, turned_ref, near_sem, across_sem, out_sem,
):
    n_zh, tok_rows, width = near_ref.shape
    halves, panels = across_ref.shape[:2]
    n_x, n_zl, sub_rows = out_ref.shape[1], out_ref.shape[3], out_ref.shape[5]
    near_copies = [
        pltpu.make_async_copy(near_any.at[z, 0:tok_rows], near_ref.at[z], near_sem.at[z])
        for z in range(n_zh)
    ]
    across_copies = [
        pltpu.make_async_copy(
            across_any.at[h * panels : (h + 1) * panels], across_ref.at[h], across_sem.at[h]
        )
        for h in range(halves)
    ]
    out_copies = [
        pltpu.make_async_copy(
            out_ref.at[h], out_any.at[:, h * panels : (h + 1) * panels], out_sem.at[h]
        )
        for h in range(halves)
    ]
    for copy in near_copies + across_copies:
        copy.start()
    token = lax.broadcasted_iota(jnp.int32, (width, tok_rows), 1)
    live = jnp.where(token < counts_ref[place_ref[0]], 1.0, 0.0).astype(BF16)
    for z in range(n_zh):
        near_copies[z].wait()
        turned_ref[z * width : (z + 1) * width, :] = near_ref[z].T * live
    for h in range(halves):
        across_copies[h].wait()
        beside = jnp.concatenate([across_ref[h, p] for p in range(panels)], axis=1)
        product = jnp.dot(turned_ref[...], beside, preferred_element_type=F32)
        for z in range(n_zh):
            for low in range(n_zl):
                for x in range(n_x):
                    row = ((z * n_zl + low) * n_x + x) * sub_rows
                    for p in range(panels):
                        out_ref[h, x, p, low, z] = product[
                            row : row + sub_rows, p * width : (p + 1) * width
                        ]
        out_copies[h].start()
    for copy in out_copies:
        copy.wait()


def tile(place, counts, near, across, n_zl, n_x, sub_rows):
    n_zh, width = near.shape[0], near.shape[2]
    panels, tok_rows = across.shape[:2]
    half = panels // 2
    smem = pl.BlockSpec(memory_space=pltpu.SMEM)
    anywhere = pl.BlockSpec(memory_space=pl.ANY)
    return pl.pallas_call(
        tile_kernel,
        out_shape=jax.ShapeDtypeStruct((n_x, panels, n_zl, n_zh, sub_rows, width), F32),
        in_specs=[smem, smem, anywhere, anywhere],
        out_specs=anywhere,
        scratch_shapes=[
            pltpu.VMEM((n_zh, tok_rows, width), BF16),
            pltpu.VMEM((2, half, tok_rows, width), BF16),
            pltpu.VMEM((2, n_x, half, n_zl, n_zh, sub_rows, width), F32),
            pltpu.VMEM((n_zh * width, tok_rows), BF16),
            pltpu.SemaphoreType.DMA((n_zh,)),
            pltpu.SemaphoreType.DMA((2,)),
            pltpu.SemaphoreType.DMA((2,)),
        ],
        name="tile",
    )(place, counts, near, across)


def local(features, sketch, counts):
    tok_rows, width = features.shape
    sub_rows, rank = sketch.shape[1:]
    n_dp, n_panel = lax.axis_size(DP), lax.axis_size(PANEL)
    n_zl, n_x, n_y, n_zh, n_c = (lax.axis_size(name) for name in DP + PANEL)
    token_total = jnp.sum(counts).astype(F32)

    high = lax.reduce_precision(sketch[0], 8, 7)
    rest = sketch[0] - high
    middle = lax.reduce_precision(rest, 8, 7)
    extra = jnp.stack([high, middle, rest - middle]).astype(BF16).reshape(-1, width)

    across = lax.all_gather(features, YC)
    along_z = lax.all_gather(jnp.concatenate([features, extra]), "zh")
    thirds = along_z[:, tok_rows:].reshape(-1, width)
    thirds = lax.all_gather(jnp.pad(thirds, ((0, PAD_ROWS - thirds.shape[0]), (0, 0))), YC)
    thirds = thirds[:, 0 : n_zh * extra.shape[0]].astype(F32)
    thirds = thirds.reshape(n_y * n_c, n_zh, 3, sub_rows, rank)
    start = (thirds[:, :, 0] + thirds[:, :, 1]) + thirds[:, :, 2]
    start = start.reshape(n_panel * sub_rows, rank)

    sums = tile(lax.axis_index(DP).reshape(1), counts, along_z, across, n_zl, n_x, sub_rows)
    sums = sums.reshape(n_x * n_y * n_c, n_zl, n_zh, sub_rows, width)
    sums = exchange(sums, XYC).reshape(n_x, n_y * n_c, n_zl, n_zh, sub_rows, width)
    sums = jnp.sum(sums, axis=0).transpose(1, 0, 2, 3, 4)
    sums = jnp.sum(exchange(sums, ("zl",)), axis=0) / token_total

    columns = sums.reshape(n_panel * sub_rows, width)
    covariance = sums.reshape(n_y, n_c, n_zh, sub_rows, width)
    covariance = covariance.transpose(4, 0, 2, 1, 3).reshape(width, 1, n_panel * sub_rows)

    product = lax.dot_general(
        columns, start, (((0,), (0,)), ((), ())), precision=HIGH, preferred_element_type=F32
    )
    product = jnp.sum(exchange(product.reshape(n_dp, sub_rows, rank), DP), axis=0)
    product = gather(product, DP).reshape(width, rank)
    product = jnp.dot(columns, product, precision=HIGH, preferred_element_type=F32)
    rows = jnp.sum(exchange(product.reshape(n_y * n_c, n_zh * sub_rows, rank), YC), axis=0)
    rows = RAISE * jnp.sum(lax.all_gather(rows, "zh"), axis=0)

    gram = lax.dot_general(
        rows, rows, (((0,), (0,)), ((), ())), precision=HIGH, preferred_element_type=F32
    )
    gram = jnp.sum(exchange(gram.reshape(n_x * n_y * n_c, -1, rank), XYC), axis=0)
    gram = jnp.sum(gather(gram, ("zl",)), axis=0)
    gram = gather(gram, XYC).reshape(rank, rank)
    place = lax.axis_index("zh").reshape(1)
    basis = solve(gram, rows, place, sub_rows, math.sqrt(width * n_panel))
    return covariance, basis[None]


def solution(mesh):
    inner = Mesh(mesh.devices.reshape(4, 4, 4, 4, 2), DP + PANEL)
    return jax.shard_map(
        local,
        mesh=inner,
        in_specs=(P(DP, PANEL), P(PANEL, DP, None), P()),
        out_specs=(P(PANEL, DP, None), P(PANEL, DP, None)),
        check_vma=False,
    )
```

```python
import functools
import math

import jax
import jax.numpy as jnp
from jax import lax
from jax.experimental import pallas as pl
from jax.experimental.pallas import tpu as pltpu
from jax.sharding import Mesh, PartitionSpec as P

F32 = jnp.float32
BF16 = jnp.bfloat16
HIGH = lax.Precision.HIGHEST
DP = ("zl", "x")
PANEL = ("y", "zh", "c")
YC = ("y", "c")
XYC = ("x", "y", "c")
RAISE = 256.0
KERNEL_VMEM = 16 * 2**20
PANEL_STEP = 64
BLOCK = 8
PAD_ROWS = 512


def exchange(blocks, axes):
    return lax.all_to_all(blocks, axes, 0, 0, tiled=True)


def gather(block, axes):
    size = lax.axis_size(axes)
    return exchange(jnp.broadcast_to(block[None], (size,) + block.shape), axes)


def solve_kernel(gram_ref, rows_ref, out_ref, held_ref, *, scale_by):
    count, rank = out_ref.shape
    width = held_ref.shape[1]
    lanes = width - rank
    own = rows_ref[pl.ds(pl.multiple_of(lax.axis_index("zh") * count, count), count), :]
    gram = gram_ref[...]
    diagonal = lax.broadcasted_iota(jnp.int32, gram.shape, 0) == lax.broadcasted_iota(
        jnp.int32, gram.shape, 1
    )
    kept = jnp.where(diagonal, gram, 0.0)
    down = 1.0 / jnp.sqrt(jnp.sum(kept, axis=1, keepdims=True))
    along = 1.0 / jnp.sqrt(jnp.sum(kept, axis=0, keepdims=True))
    own = jnp.concatenate([own * along, jnp.zeros((lanes - count, rank), F32)], axis=0)
    held_ref[:, 0:rank] = gram * down * along
    held_ref[:, rank:width] = own.T
    for first in range(0, rank, PANEL_STEP):
        last = first + PANEL_STEP
        parts = {}
        for at in range(first // lanes * lanes, width, lanes):
            parts[at] = held_ref[first:last, at : at + lanes]
            if first > 0:
                parts[at] = parts[at] - lax.dot_general(
                    held_ref[0:first, first:last],
                    held_ref[0:first, at : at + lanes],
                    (((0,), (0,)), ((), ())),
                    precision=HIGH,
                    preferred_element_type=F32,
                )
        for pivot in range(first, last, BLOCK):
            base = pivot // lanes * lanes
            parts = {at: part for at, part in parts.items() if at >= base}
            source, lane = parts[base], pivot - base
            columns = [
                jnp.broadcast_to(source[:, lane + j : lane + j + 1], source.shape)
                for j in range(BLOCK)
            ]
            square = [[columns[j][i : i + 1] for j in range(i + 1)] for i in range(BLOCK)]
            rows = [{at: part[j : j + 1] for at, part in parts.items()} for j in range(BLOCK)]
            inverse = []
            for j in range(BLOCK):
                if j % 2 == 0:
                    top, cross, corner = square[j][j], square[j + 1][j], square[j + 1][j + 1]
                    inverse.append(1.0 / top)
                    inverse.append(top * (1.0 / (top * corner - cross * cross)))
                for i in range(j + 1, BLOCK):
                    factor = square[i][j] * inverse[j]
                    for m in range(j + 1, i + 1):
                        square[i][m] = square[i][m] - factor * square[m][j]
                    for at in parts:
                        rows[i][at] = rows[i][at] - factor * rows[j][at]
                    if pivot + BLOCK < last:
                        columns[i] = columns[i] - columns[j] * factor
            for j in range(BLOCK):
                scale = 1.0 / jnp.sqrt(square[j][j])
                for at in parts:
                    held_ref[pivot + j : pivot + j + 1, at : at + lanes] = rows[j][at] * scale
            if pivot + BLOCK < last:
                for at in parts:
                    rest = parts[at][BLOCK:]
                    for j in range(BLOCK):
                        rest = rest - columns[j][BLOCK:] * (rows[j][at] * inverse[j])
                    parts[at] = rest
    out_ref[...] = held_ref[:, rank:width].T[0:count] * scale_by


def solve(gram, rows, count, scale_by):
    rank = rows.shape[1]
    vmem = pl.BlockSpec(memory_space=pltpu.VMEM)
    return pl.pallas_call(
        functools.partial(solve_kernel, scale_by=scale_by),
        out_shape=jax.ShapeDtypeStruct((count, rank), F32),
        in_specs=[vmem, vmem],
        out_specs=vmem,
        scratch_shapes=[pltpu.VMEM((rank, rank + 128), F32)],
        compiler_params=pltpu.CompilerParams(vmem_limit_bytes=KERNEL_VMEM),
        name="solve",
    )(gram, rows)


def tile_kernel(
    counts_any, near_any, across_any, out_any,
    counts_ref, near_ref, across_ref, out_ref, turned_ref, counts_sem, near_sem, across_sem, out_sem,
):
    n_zh, tok_rows, width = near_ref.shape
    halves, panels = across_ref.shape[:2]
    n_x, n_zl, sub_rows = out_ref.shape[1], out_ref.shape[3], out_ref.shape[5]
    near_copies = [
        pltpu.make_async_copy(near_any.at[z, 0:tok_rows], near_ref.at[z], near_sem.at[z])
        for z in range(n_zh)
    ]
    across_copies = [
        pltpu.make_async_copy(
            across_any.at[h * panels : (h + 1) * panels], across_ref.at[h], across_sem.at[h]
        )
        for h in range(halves)
    ]
    out_copies = [
        pltpu.make_async_copy(
            out_ref.at[h], out_any.at[:, h * panels : (h + 1) * panels], out_sem.at[h]
        )
        for h in range(halves)
    ]
    counts_copy = pltpu.make_async_copy(counts_any, counts_ref, counts_sem)
    for copy in [counts_copy] + near_copies + across_copies:
        copy.start()
    counts_copy.wait()
    token = lax.broadcasted_iota(jnp.int32, (width, tok_rows), 1)
    live = jnp.where(token < counts_ref[lax.axis_index(DP)], 1.0, 0.0).astype(BF16)
    for z in range(n_zh):
        near_copies[z].wait()
        turned_ref[z * width : (z + 1) * width, :] = near_ref[z].T * live
    for h in range(halves):
        across_copies[h].wait()
        beside = jnp.concatenate([across_ref[h, p] for p in range(panels)], axis=1)
        product = jnp.dot(turned_ref[...], beside, preferred_element_type=F32)
        for z in range(n_zh):
            for low in range(n_zl):
                for x in range(n_x):
                    row = ((z * n_zl + low) * n_x + x) * sub_rows
                    for p in range(panels):
                        out_ref[h, x, p, low, z] = product[
                            row : row + sub_rows, p * width : (p + 1) * width
                        ]
        out_copies[h].start()
    for copy in out_copies:
        copy.wait()


def tile(counts, near, across, n_zl, n_x, sub_rows):
    n_zh, width = near.shape[0], near.shape[2]
    panels, tok_rows = across.shape[:2]
    half = panels // 2
    anywhere = pl.BlockSpec(memory_space=pl.ANY)
    return pl.pallas_call(
        tile_kernel,
        out_shape=jax.ShapeDtypeStruct((n_x, panels, n_zl, n_zh, sub_rows, width), F32),
        in_specs=[anywhere, anywhere, anywhere],
        out_specs=anywhere,
        scratch_shapes=[
            pltpu.SMEM(counts.shape, jnp.int32),
            pltpu.VMEM((n_zh, tok_rows, width), BF16),
            pltpu.VMEM((2, half, tok_rows, width), BF16),
            pltpu.VMEM((2, n_x, half, n_zl, n_zh, sub_rows, width), F32),
            pltpu.VMEM((n_zh * width, tok_rows), BF16),
            pltpu.SemaphoreType.DMA,
            pltpu.SemaphoreType.DMA((n_zh,)),
            pltpu.SemaphoreType.DMA((2,)),
            pltpu.SemaphoreType.DMA((2,)),
        ],
        name="tile",
    )(counts, near, across)


def local(features, sketch, counts):
    tok_rows, width = features.shape
    sub_rows, rank = sketch.shape[1:]
    n_dp, n_panel = lax.axis_size(DP), lax.axis_size(PANEL)
    n_zl, n_x, n_y, n_zh, n_c = (lax.axis_size(name) for name in DP + PANEL)
    token_total = jnp.sum(counts).astype(F32)

    high = lax.reduce_precision(sketch[0], 8, 7)
    rest = sketch[0] - high
    middle = lax.reduce_precision(rest, 8, 7)
    extra = jnp.stack([high, middle, rest - middle]).astype(BF16).reshape(-1, width)

    across = lax.all_gather(features, YC)
    along_z = lax.all_gather(jnp.concatenate([features, extra]), "zh")
    thirds = along_z[:, tok_rows:].reshape(-1, width)
    thirds = lax.all_gather(jnp.pad(thirds, ((0, PAD_ROWS - thirds.shape[0]), (0, 0))), YC)
    thirds = thirds[:, 0 : n_zh * extra.shape[0]].astype(F32)
    thirds = thirds.reshape(n_y * n_c, n_zh, 3, sub_rows, rank)
    start = (thirds[:, :, 0] + thirds[:, :, 1]) + thirds[:, :, 2]
    start = start.reshape(n_panel * sub_rows, rank)

    sums = tile(counts, along_z, across, n_zl, n_x, sub_rows)
    sums = sums.reshape(n_x * n_y * n_c, n_zl, n_zh, sub_rows, width)
    sums = exchange(sums, XYC).reshape(n_x, n_y * n_c, n_zl, n_zh, sub_rows, width)
    sums = jnp.sum(sums, axis=0).transpose(1, 0, 2, 3, 4)
    sums = jnp.sum(exchange(sums, ("zl",)), axis=0) / token_total

    columns = sums.reshape(n_panel * sub_rows, width)
    covariance = sums.reshape(n_y, n_c, n_zh, sub_rows, width)
    covariance = covariance.transpose(4, 0, 2, 1, 3).reshape(width, 1, n_panel * sub_rows)

    product = lax.dot_general(
        columns, start, (((0,), (0,)), ((), ())), precision=HIGH, preferred_element_type=F32
    )
    product = jnp.sum(exchange(product.reshape(n_dp, sub_rows, rank), DP), axis=0)
    product = gather(product, DP).reshape(width, rank)
    product = jnp.dot(columns, product, precision=HIGH, preferred_element_type=F32)
    rows = jnp.sum(exchange(product.reshape(n_y * n_c, n_zh * sub_rows, rank), YC), axis=0)
    rows = RAISE * jnp.sum(lax.all_gather(rows, "zh"), axis=0)

    gram = lax.dot_general(
        rows, rows, (((0,), (0,)), ((), ())), precision=HIGH, preferred_element_type=F32
    )
    gram = jnp.sum(exchange(gram.reshape(n_x * n_y * n_c, -1, rank), XYC), axis=0)
    gram = jnp.sum(gather(gram, ("zl",)), axis=0)
    gram = gather(gram, XYC).reshape(rank, rank)
    basis = solve(gram, rows, sub_rows, math.sqrt(width * n_panel))
    return covariance, basis[None]


def solution(mesh):
    inner = Mesh(mesh.devices.reshape(4, 4, 4, 4, 2), DP + PANEL)
    return jax.shard_map(
        local,
        mesh=inner,
        in_specs=(P(DP, PANEL), P(PANEL, DP, None), P()),
        out_specs=(P(PANEL, DP, None), P(PANEL, DP, None)),
        check_vma=False,
    )
```

```python
import functools
import math

import jax
import jax.numpy as jnp
from jax import lax
from jax.experimental import pallas as pl
from jax.experimental.pallas import tpu as pltpu
from jax.sharding import Mesh, PartitionSpec as P

F32 = jnp.float32
BF16 = jnp.bfloat16
HIGH = lax.Precision.HIGHEST
DP = ("zl", "x")
PANEL = ("y", "zh", "c")
CY = ("c", "y")
XCY = ("x", "c", "y")
RAISE = 256.0
KERNEL_VMEM = 16 * 2**20
PANEL_STEP = 64
BLOCK = 8
PAD_ROWS = 512


def exchange(blocks, axes):
    return lax.all_to_all(blocks, axes, 0, 0, tiled=True)


def gather(block, axes):
    size = lax.axis_size(axes)
    return exchange(jnp.broadcast_to(block[None], (size,) + block.shape), axes)


def solve_kernel(gram_ref, rows_ref, out_ref, held_ref, *, scale_by):
    count, rank = out_ref.shape
    width = held_ref.shape[1]
    lanes = width - rank
    own = rows_ref[pl.ds(pl.multiple_of(lax.axis_index("zh") * count, count), count), :]
    gram = gram_ref[...]
    diagonal = lax.broadcasted_iota(jnp.int32, gram.shape, 0) == lax.broadcasted_iota(
        jnp.int32, gram.shape, 1
    )
    kept = jnp.where(diagonal, gram, 0.0)
    down = 1.0 / jnp.sqrt(jnp.sum(kept, axis=1, keepdims=True))
    along = 1.0 / jnp.sqrt(jnp.sum(kept, axis=0, keepdims=True))
    own = jnp.concatenate([own * along, jnp.zeros((lanes - count, rank), F32)], axis=0)
    held_ref[:, 0:rank] = gram * down * along
    held_ref[:, rank:width] = own.T
    for first in range(0, rank, PANEL_STEP):
        last = first + PANEL_STEP
        parts = {}
        for at in range(first // lanes * lanes, width, lanes):
            parts[at] = held_ref[first:last, at : at + lanes]
            if first > 0:
                parts[at] = parts[at] - lax.dot_general(
                    held_ref[0:first, first:last],
                    held_ref[0:first, at : at + lanes],
                    (((0,), (0,)), ((), ())),
                    precision=HIGH,
                    preferred_element_type=F32,
                )
        for pivot in range(first, last, BLOCK):
            base = pivot // lanes * lanes
            parts = {at: part for at, part in parts.items() if at >= base}
            source, lane = parts[base], pivot - base
            columns = [
                jnp.broadcast_to(source[:, lane + j : lane + j + 1], source.shape)
                for j in range(BLOCK)
            ]
            square = [[columns[j][i : i + 1] for j in range(i + 1)] for i in range(BLOCK)]
            rows = [{at: part[j : j + 1] for at, part in parts.items()} for j in range(BLOCK)]
            inverse = []
            for j in range(BLOCK):
                if j % 2 == 0:
                    top, cross, corner = square[j][j], square[j + 1][j], square[j + 1][j + 1]
                    inverse.append(1.0 / top)
                    inverse.append(top * (1.0 / (top * corner - cross * cross)))
                for i in range(j + 1, BLOCK):
                    factor = square[i][j] * inverse[j]
                    for m in range(j + 1, i + 1):
                        square[i][m] = square[i][m] - factor * square[m][j]
                    for at in parts:
                        rows[i][at] = rows[i][at] - factor * rows[j][at]
                    if pivot + BLOCK < last:
                        columns[i] = columns[i] - columns[j] * factor
            for j in range(BLOCK):
                scale = 1.0 / jnp.sqrt(square[j][j])
                for at in parts:
                    held_ref[pivot + j : pivot + j + 1, at : at + lanes] = rows[j][at] * scale
            if pivot + BLOCK < last:
                for at in parts:
                    rest = parts[at][BLOCK:]
                    for j in range(BLOCK):
                        rest = rest - columns[j][BLOCK:] * (rows[j][at] * inverse[j])
                    parts[at] = rest
    out_ref[...] = held_ref[:, rank:width].T[0:count] * scale_by


def solve(gram, rows, count, scale_by):
    rank = rows.shape[1]
    vmem = pl.BlockSpec(memory_space=pltpu.VMEM)
    return pl.pallas_call(
        functools.partial(solve_kernel, scale_by=scale_by),
        out_shape=jax.ShapeDtypeStruct((count, rank), F32),
        in_specs=[vmem, vmem],
        out_specs=vmem,
        scratch_shapes=[pltpu.VMEM((rank, rank + 128), F32)],
        compiler_params=pltpu.CompilerParams(vmem_limit_bytes=KERNEL_VMEM),
        name="solve",
    )(gram, rows)


def tile_kernel(
    counts_any, near_any, across_any, out_any,
    counts_ref, near_ref, across_ref, out_ref, turned_ref, counts_sem, near_sem, across_sem, out_sem,
):
    n_zh, tok_rows, width = near_ref.shape
    halves, panels = across_ref.shape[:2]
    n_x, n_zl, sub_rows = out_ref.shape[1], out_ref.shape[3], out_ref.shape[5]
    near_copies = [
        pltpu.make_async_copy(near_any.at[z, 0:tok_rows], near_ref.at[z], near_sem.at[z])
        for z in range(n_zh)
    ]
    across_copies = [
        pltpu.make_async_copy(
            across_any.at[h * panels : (h + 1) * panels], across_ref.at[h], across_sem.at[h]
        )
        for h in range(halves)
    ]
    out_copies = [
        pltpu.make_async_copy(
            out_ref.at[h], out_any.at[:, h * panels : (h + 1) * panels], out_sem.at[h]
        )
        for h in range(halves)
    ]
    counts_copy = pltpu.make_async_copy(counts_any, counts_ref, counts_sem)
    for copy in [counts_copy] + near_copies + across_copies:
        copy.start()
    counts_copy.wait()
    token = lax.broadcasted_iota(jnp.int32, (width, tok_rows), 1)
    live = jnp.where(token < counts_ref[lax.axis_index(DP)], 1.0, 0.0).astype(BF16)
    for z in range(n_zh):
        near_copies[z].wait()
        turned_ref[z * width : (z + 1) * width, :] = near_ref[z].T * live
    for h in range(halves):
        across_copies[h].wait()
        beside = jnp.concatenate([across_ref[h, p] for p in range(panels)], axis=1)
        product = jnp.dot(turned_ref[...], beside, preferred_element_type=F32)
        for z in range(n_zh):
            for low in range(n_zl):
                for x in range(n_x):
                    row = ((z * n_zl + low) * n_x + x) * sub_rows
                    for p in range(panels):
                        out_ref[h, x, p, low, z] = product[
                            row : row + sub_rows, p * width : (p + 1) * width
                        ]
        out_copies[h].start()
    for copy in out_copies:
        copy.wait()


def tile(counts, near, across, n_zl, n_x, sub_rows):
    n_zh, width = near.shape[0], near.shape[2]
    panels, tok_rows = across.shape[:2]
    half = panels // 2
    anywhere = pl.BlockSpec(memory_space=pl.ANY)
    return pl.pallas_call(
        tile_kernel,
        out_shape=jax.ShapeDtypeStruct((n_x, panels, n_zl, n_zh, sub_rows, width), F32),
        in_specs=[anywhere, anywhere, anywhere],
        out_specs=anywhere,
        scratch_shapes=[
            pltpu.SMEM(counts.shape, jnp.int32),
            pltpu.VMEM((n_zh, tok_rows, width), BF16),
            pltpu.VMEM((2, half, tok_rows, width), BF16),
            pltpu.VMEM((2, n_x, half, n_zl, n_zh, sub_rows, width), F32),
            pltpu.VMEM((n_zh * width, tok_rows), BF16),
            pltpu.SemaphoreType.DMA,
            pltpu.SemaphoreType.DMA((n_zh,)),
            pltpu.SemaphoreType.DMA((2,)),
            pltpu.SemaphoreType.DMA((2,)),
        ],
        name="tile",
    )(counts, near, across)


def local(features, sketch, counts):
    tok_rows, width = features.shape
    sub_rows, rank = sketch.shape[1:]
    n_dp, n_panel = lax.axis_size(DP), lax.axis_size(PANEL)
    n_zl, n_x, n_y, n_zh, n_c = (lax.axis_size(name) for name in DP + PANEL)
    token_total = jnp.sum(counts).astype(F32)

    high = lax.reduce_precision(sketch[0], 8, 7)
    rest = sketch[0] - high
    middle = lax.reduce_precision(rest, 8, 7)
    extra = jnp.stack([high, middle, rest - middle]).astype(BF16).reshape(-1, width)

    across = lax.all_gather(features, CY)
    along_z = lax.all_gather(jnp.concatenate([features, extra]), "zh")
    thirds = along_z[:, tok_rows:].reshape(-1, width)
    thirds = lax.all_gather(jnp.pad(thirds, ((0, PAD_ROWS - thirds.shape[0]), (0, 0))), CY)
    thirds = thirds[:, 0 : n_zh * extra.shape[0]].astype(F32)
    thirds = thirds.reshape(n_y * n_c, n_zh, 3, sub_rows, rank)
    start = (thirds[:, :, 0] + thirds[:, :, 1]) + thirds[:, :, 2]
    start = start.reshape(n_panel * sub_rows, rank)

    sums = tile(counts, along_z, across, n_zl, n_x, sub_rows)
    sums = sums.reshape(n_x * n_y * n_c, n_zl, n_zh, sub_rows, width)
    sums = exchange(sums, XCY).reshape(n_x, n_y * n_c, n_zl, n_zh, sub_rows, width)
    sums = jnp.sum(sums, axis=0).transpose(1, 0, 2, 3, 4)
    sums = jnp.sum(exchange(sums, ("zl",)), axis=0) / token_total

    columns = sums.reshape(n_panel * sub_rows, width)
    covariance = sums.reshape(n_c, n_y, n_zh, sub_rows, width)
    covariance = covariance.transpose(4, 1, 2, 0, 3).reshape(width, 1, n_panel * sub_rows)

    product = lax.dot_general(
        columns, start, (((0,), (0,)), ((), ())), precision=HIGH, preferred_element_type=F32
    )
    product = jnp.sum(exchange(product.reshape(n_dp, sub_rows, rank), DP), axis=0)
    product = gather(product, DP).reshape(width, rank)
    product = jnp.dot(columns, product, precision=HIGH, preferred_element_type=F32)
    rows = jnp.sum(exchange(product.reshape(n_y * n_c, n_zh * sub_rows, rank), CY), axis=0)
    rows = RAISE * jnp.sum(lax.all_gather(rows, "zh"), axis=0)

    gram = lax.dot_general(
        rows, rows, (((0,), (0,)), ((), ())), precision=HIGH, preferred_element_type=F32
    )
    gram = jnp.sum(exchange(gram.reshape(n_x * n_y * n_c, -1, rank), XCY), axis=0)
    gram = jnp.sum(gather(gram, ("zl",)), axis=0)
    gram = gather(gram, XCY).reshape(rank, rank)
    basis = solve(gram, rows, sub_rows, math.sqrt(width * n_panel))
    return covariance, basis[None]


def solution(mesh):
    inner = Mesh(mesh.devices.reshape(4, 4, 4, 4, 2), DP + PANEL)
    return jax.shard_map(
        local,
        mesh=inner,
        in_specs=(P(DP, PANEL), P(PANEL, DP, None), P()),
        out_specs=(P(PANEL, DP, None), P(PANEL, DP, None)),
        check_vma=False,
    )
```

```python
import functools
import math

import jax
import jax.numpy as jnp
from jax import lax
from jax.experimental import pallas as pl
from jax.experimental.pallas import tpu as pltpu
from jax.sharding import Mesh, PartitionSpec as P

F32 = jnp.float32
BF16 = jnp.bfloat16
HIGH = lax.Precision.HIGHEST
DP = ("zl", "x")
PANEL = ("y", "zh", "c")
CY = ("c", "y")
XZ = ("x", "zl")
XCY = ("x", "c", "y")
RAISE = 256.0
KERNEL_VMEM = 16 * 2**20
PANEL_STEP = 64
BLOCK = 8
PAD_ROWS = 512


def exchange(blocks, axes):
    return lax.all_to_all(blocks, axes, 0, 0, tiled=True)


def gather(block, axes):
    size = lax.axis_size(axes)
    return exchange(jnp.broadcast_to(block[None], (size,) + block.shape), axes)


def solve_kernel(gram_ref, rows_ref, out_ref, held_ref, *, scale_by):
    count, rank = out_ref.shape
    width = held_ref.shape[1]
    lanes = width - rank
    own = rows_ref[pl.ds(pl.multiple_of(lax.axis_index("zh") * count, count), count), :]
    gram = gram_ref[...]
    diagonal = lax.broadcasted_iota(jnp.int32, gram.shape, 0) == lax.broadcasted_iota(
        jnp.int32, gram.shape, 1
    )
    kept = jnp.where(diagonal, gram, 0.0)
    down = 1.0 / jnp.sqrt(jnp.sum(kept, axis=1, keepdims=True))
    along = 1.0 / jnp.sqrt(jnp.sum(kept, axis=0, keepdims=True))
    own = jnp.concatenate([own * along, jnp.zeros((lanes - count, rank), F32)], axis=0)
    held_ref[:, 0:rank] = gram * down * along
    held_ref[:, rank:width] = own.T
    for first in range(0, rank, PANEL_STEP):
        last = first + PANEL_STEP
        parts = {}
        for at in range(first // lanes * lanes, width, lanes):
            parts[at] = held_ref[first:last, at : at + lanes]
            if first > 0:
                parts[at] = parts[at] - lax.dot_general(
                    held_ref[0:first, first:last],
                    held_ref[0:first, at : at + lanes],
                    (((0,), (0,)), ((), ())),
                    precision=HIGH,
                    preferred_element_type=F32,
                )
        for pivot in range(first, last, BLOCK):
            base = pivot // lanes * lanes
            parts = {at: part for at, part in parts.items() if at >= base}
            source, lane = parts[base], pivot - base
            columns = [
                jnp.broadcast_to(source[:, lane + j : lane + j + 1], source.shape)
                for j in range(BLOCK)
            ]
            square = [[columns[j][i : i + 1] for j in range(i + 1)] for i in range(BLOCK)]
            rows = [{at: part[j : j + 1] for at, part in parts.items()} for j in range(BLOCK)]
            inverse = []
            for j in range(BLOCK):
                if j % 2 == 0:
                    top, cross, corner = square[j][j], square[j + 1][j], square[j + 1][j + 1]
                    inverse.append(1.0 / top)
                    inverse.append(top * (1.0 / (top * corner - cross * cross)))
                for i in range(j + 1, BLOCK):
                    factor = square[i][j] * inverse[j]
                    for m in range(j + 1, i + 1):
                        square[i][m] = square[i][m] - factor * square[m][j]
                    for at in parts:
                        rows[i][at] = rows[i][at] - factor * rows[j][at]
                    if pivot + BLOCK < last:
                        columns[i] = columns[i] - columns[j] * factor
            for j in range(BLOCK):
                scale = 1.0 / jnp.sqrt(square[j][j])
                for at in parts:
                    held_ref[pivot + j : pivot + j + 1, at : at + lanes] = rows[j][at] * scale
            if pivot + BLOCK < last:
                for at in parts:
                    rest = parts[at][BLOCK:]
                    for j in range(BLOCK):
                        rest = rest - columns[j][BLOCK:] * (rows[j][at] * inverse[j])
                    parts[at] = rest
    out_ref[...] = held_ref[:, rank:width].T[0:count] * scale_by


def solve(gram, rows, count, scale_by):
    rank = rows.shape[1]
    vmem = pl.BlockSpec(memory_space=pltpu.VMEM)
    return pl.pallas_call(
        functools.partial(solve_kernel, scale_by=scale_by),
        out_shape=jax.ShapeDtypeStruct((count, rank), F32),
        in_specs=[vmem, vmem],
        out_specs=vmem,
        scratch_shapes=[pltpu.VMEM((rank, rank + 128), F32)],
        compiler_params=pltpu.CompilerParams(vmem_limit_bytes=KERNEL_VMEM),
        name="solve",
    )(gram, rows)


def tile_kernel(
    counts_any, near_any, across_any, out_any,
    counts_ref, near_ref, across_ref, out_ref, turned_ref, counts_sem, near_sem, across_sem, out_sem,
):
    n_zh, tok_rows, width = near_ref.shape
    halves, panels = across_ref.shape[:2]
    n_x, n_zl, sub_rows = out_ref.shape[1], out_ref.shape[3], out_ref.shape[5]
    near_copies = [
        pltpu.make_async_copy(near_any.at[z, 0:tok_rows], near_ref.at[z], near_sem.at[z])
        for z in range(n_zh)
    ]
    across_copies = [
        pltpu.make_async_copy(
            across_any.at[h * panels : (h + 1) * panels], across_ref.at[h], across_sem.at[h]
        )
        for h in range(halves)
    ]
    out_copies = [
        pltpu.make_async_copy(
            out_ref.at[h], out_any.at[:, h * panels : (h + 1) * panels], out_sem.at[h]
        )
        for h in range(halves)
    ]
    counts_copy = pltpu.make_async_copy(counts_any, counts_ref, counts_sem)
    for copy in [counts_copy] + near_copies + across_copies:
        copy.start()
    counts_copy.wait()
    token = lax.broadcasted_iota(jnp.int32, (width, tok_rows), 1)
    live = jnp.where(token < counts_ref[lax.axis_index(DP)], 1.0, 0.0).astype(BF16)
    for z in range(n_zh):
        near_copies[z].wait()
        turned_ref[z * width : (z + 1) * width, :] = near_ref[z].T * live
    for h in range(halves):
        across_copies[h].wait()
        beside = jnp.concatenate([across_ref[h, p] for p in range(panels)], axis=1)
        product = jnp.dot(turned_ref[...], beside, preferred_element_type=F32)
        for z in range(n_zh):
            for low in range(n_zl):
                for x in range(n_x):
                    row = ((z * n_zl + low) * n_x + x) * sub_rows
                    for p in range(panels):
                        out_ref[h, x, p, low, z] = product[
                            row : row + sub_rows, p * width : (p + 1) * width
                        ]
        out_copies[h].start()
    for copy in out_copies:
        copy.wait()


def tile(counts, near, across, n_zl, n_x, sub_rows):
    n_zh, width = near.shape[0], near.shape[2]
    panels, tok_rows = across.shape[:2]
    half = panels // 2
    anywhere = pl.BlockSpec(memory_space=pl.ANY)
    return pl.pallas_call(
        tile_kernel,
        out_shape=jax.ShapeDtypeStruct((n_x, panels, n_zl, n_zh, sub_rows, width), F32),
        in_specs=[anywhere, anywhere, anywhere],
        out_specs=anywhere,
        scratch_shapes=[
            pltpu.SMEM(counts.shape, jnp.int32),
            pltpu.VMEM((n_zh, tok_rows, width), BF16),
            pltpu.VMEM((2, half, tok_rows, width), BF16),
            pltpu.VMEM((2, n_x, half, n_zl, n_zh, sub_rows, width), F32),
            pltpu.VMEM((n_zh * width, tok_rows), BF16),
            pltpu.SemaphoreType.DMA,
            pltpu.SemaphoreType.DMA((n_zh,)),
            pltpu.SemaphoreType.DMA((2,)),
            pltpu.SemaphoreType.DMA((2,)),
        ],
        name="tile",
    )(counts, near, across)


def local(features, sketch, counts):
    tok_rows, width = features.shape
    sub_rows, rank = sketch.shape[1:]
    n_dp, n_panel = lax.axis_size(DP), lax.axis_size(PANEL)
    n_zl, n_x, n_y, n_zh, n_c = (lax.axis_size(name) for name in DP + PANEL)
    token_total = jnp.sum(counts).astype(F32)

    high = lax.reduce_precision(sketch[0], 8, 7)
    rest = sketch[0] - high
    middle = lax.reduce_precision(rest, 8, 7)
    extra = jnp.stack([high, middle, rest - middle]).astype(BF16).reshape(-1, width)

    across = lax.all_gather(features, CY)
    along_z = lax.all_gather(jnp.concatenate([features, extra]), "zh")
    thirds = along_z[:, tok_rows:].reshape(-1, width)
    thirds = lax.all_gather(jnp.pad(thirds, ((0, PAD_ROWS - thirds.shape[0]), (0, 0))), CY)
    thirds = thirds[:, 0 : n_zh * extra.shape[0]].astype(F32)
    thirds = thirds.reshape(n_y * n_c, n_zh, 3, sub_rows, rank)
    start = (thirds[:, :, 0] + thirds[:, :, 1]) + thirds[:, :, 2]
    start = start.reshape(n_panel * sub_rows, rank)

    sums = tile(counts, along_z, across, n_zl, n_x, sub_rows)
    sums = sums.reshape(n_x * n_y * n_c, n_zl, n_zh, sub_rows, width)
    sums = exchange(sums, XCY).reshape(n_x, n_y * n_c, n_zl, n_zh, sub_rows, width)
    sums = jnp.sum(sums, axis=0).transpose(1, 0, 2, 3, 4)
    sums = jnp.sum(exchange(sums, ("zl",)), axis=0) / token_total

    columns = sums.reshape(n_panel * sub_rows, width)
    covariance = sums.reshape(n_c, n_y, n_zh, sub_rows, width)
    covariance = covariance.transpose(4, 1, 2, 0, 3).reshape(width, 1, n_panel * sub_rows)

    product = lax.dot_general(
        columns, start, (((0,), (0,)), ((), ())), precision=HIGH, preferred_element_type=F32
    )
    product = product.reshape(n_zl, n_x, sub_rows, rank).transpose(1, 0, 2, 3)
    product = jnp.sum(exchange(product.reshape(n_dp, sub_rows, rank), XZ), axis=0)
    product = gather(product, XZ).reshape(n_x, n_zl, sub_rows, rank).transpose(1, 0, 2, 3)
    product = product.reshape(width, rank)
    product = jnp.dot(columns, product, precision=HIGH, preferred_element_type=F32)
    rows = jnp.sum(exchange(product.reshape(n_y * n_c, n_zh * sub_rows, rank), CY), axis=0)
    rows = RAISE * jnp.sum(lax.all_gather(rows, "zh"), axis=0)

    gram = lax.dot_general(
        rows, rows, (((0,), (0,)), ((), ())), precision=HIGH, preferred_element_type=F32
    )
    gram = jnp.sum(exchange(gram.reshape(n_x * n_y * n_c, -1, rank), XCY), axis=0)
    gram = jnp.sum(gather(gram, ("zl",)), axis=0)
    gram = gather(gram, XCY).reshape(rank, rank)
    basis = solve(gram, rows, sub_rows, math.sqrt(width * n_panel))
    return covariance, basis[None]


def solution(mesh):
    inner = Mesh(mesh.devices.reshape(4, 4, 4, 4, 2), DP + PANEL)
    return jax.shard_map(
        local,
        mesh=inner,
        in_specs=(P(DP, PANEL), P(PANEL, DP, None), P()),
        out_specs=(P(PANEL, DP, None), P(PANEL, DP, None)),
        check_vma=False,
    )
```
